32 devices in a mesh: ha: 2 (over x), wa: 16 (over z, y, core).
Axes of the slice: x: 2, y: 2, z: 4, core: 2. Of those that a mesh axis runs over, the one named last changes fastest.
Arguments:
- queries: float32 [2, 16, 128, 256], P(None, 'ha', 'wa'), may hold values from -240 to 240
- keys: float32 [2, 16, 128, 256], P(None, 'ha', 'wa'), may hold values from -6 to 6
- values: float32 [2, 16, 128, 256], P(None, 'ha', 'wa'), may hold values from -6 to 6
- cotangent: float32 [2, 16, 128, 256], P(None, 'ha', 'wa'), may hold values from -6 to 6
Outputs:
- query_grad: float32 [2, 16, 128, 256], P(None, 'ha', 'wa')
- key_grad: float32 [2, 16, 128, 256], P(None, 'ha', 'wa')
- value_grad: float32 [2, 16, 128, 256], P(None, 'ha', 'wa')
The draws below stay inside these ranges and needn't reach their ends.
All inputs are finite; a program needn't handle non-finite values.
Results may differ from the reference program's by a relative error of at most 0.0003.
Values sent between devices are 32-bit elements; how exact they have to be, the bound alone decides.
No kernel may reach another device: no remote copies, remote signals or barrier semaphores. Data moves between devices by JAX's collectives and lax.ppermute only.
A program may use at most 128 MiB of HBM per device.

```python
import math
import jax
import jax.numpy as jnp
from jax import lax

HEADS = 4
HEAD_DIM = 64
CHANNELS = 256
IMAGES = 2
GRID_ROWS = 16
GRID_COLS = 128


def shared_fields(key):
    shape = (IMAGES, GRID_ROWS, GRID_COLS, CHANNELS)
    basis = jnp.clip(jax.random.normal(jax.random.fold_in(key, 11), shape, jnp.float32), -6.0, 6.0)
    return basis


def draw_keys(key, part):
    basis = shared_fields(key)
    return basis


def draw_queries(key, part):
    shape = (IMAGES, GRID_ROWS, GRID_COLS, CHANNELS)
    fresh = jnp.clip(jax.random.normal(jax.random.fold_in(key, 15), shape, jnp.float32), -6.0, 6.0)
    return fresh


def levels(stream_key, shape, cuts, least, top_value):
    gain = 1.0
    for dim, blocks in cuts:
        draws = jax.random.uniform(jax.random.fold_in(jax.random.fold_in(stream_key, 6), dim), (blocks,), jnp.float32, least / len(cuts), top_value / len(cuts))
        gain = gain * jnp.repeat(jnp.exp(draws), shape[dim] // blocks).reshape((-1,) + (1,) * (len(shape) - 1 - dim))
    return gain


def bell_draw(own_key, shape, deviation, most, pieces=(), kind=jnp.bfloat16):
    values = jax.random.normal(own_key, shape, jnp.float32) * deviation
    if len(pieces) > 0:
        values = levels(own_key, shape, pieces, -0.22, 0.18) * values
    return jnp.clip(values, min=-most, max=most).astype(kind)


def setup_inputs(seed: int = 0) -> dict:
    streams_of = jax.random.split(jax.random.key(seed), 5)
    return {
        "queries": draw_queries(jax.random.fold_in(streams_of[4], 71), 0),
        "keys": draw_keys(jax.random.fold_in(streams_of[4], 71), 0),
        "values": bell_draw(streams_of[2], (IMAGES, GRID_ROWS, GRID_COLS, CHANNELS), 1.0, 6.0, ((1, 2), (2, 16)), jnp.float32),
        "cotangent": bell_draw(streams_of[3], (IMAGES, GRID_ROWS, GRID_COLS, CHANNELS), 1.0, 6.0, ((1, 2), (2, 16)), jnp.float32),
    }


def single_image(queries, keys, values, cotangent):
    grid_rows = queries.shape[0]
    grid_cols = queries.shape[1]
    scale = 1.0 / math.sqrt(HEAD_DIM)
    split = (grid_rows, grid_cols, HEADS, HEAD_DIM)
    query_heads = queries.reshape(split)
    cot_heads = cotangent.reshape(split)
    widths = ((3, 3), (3, 3), (0, 0), (0, 0))
    key_pad = jnp.pad(keys.reshape(split), widths)
    value_pad = jnp.pad(values.reshape(split), widths)
    inside = jnp.pad(jnp.ones((grid_rows, grid_cols), dtype=bool), 3)
    offsets = [(row_off, col_off) for row_off in range(7) for col_off in range(7)]
    score_list = []
    for row_off, col_off in offsets:
        shifted = key_pad[row_off:row_off + grid_rows, col_off:col_off + grid_cols]
        score = lax.optimization_barrier(jnp.sum(query_heads * shifted, axis=-1)) * scale
        live = inside[row_off:row_off + grid_rows, col_off:col_off + grid_cols][:, :, None]
        score_list.append(jnp.where(live, score, -jnp.inf))
    scores = jnp.stack(score_list)
    top = lax.optimization_barrier(jnp.max(scores, axis=0))
    expd = jnp.exp(scores - top[None])
    probs = expd / lax.optimization_barrier(jnp.sum(expd, axis=0))[None]
    attended = jnp.zeros(split, jnp.float32)
    for index, (row_off, col_off) in enumerate(offsets):
        shifted = value_pad[row_off:row_off + grid_rows, col_off:col_off + grid_cols]
        attended = attended + probs[index][..., None] * shifted
    delta = lax.optimization_barrier(jnp.sum(cot_heads * attended, axis=-1))
    query_grad = jnp.zeros(split, jnp.float32)
    key_acc = jnp.zeros(key_pad.shape, jnp.float32)
    value_acc = jnp.zeros(value_pad.shape, jnp.float32)
    for index, (row_off, col_off) in enumerate(offsets):
        vshift = value_pad[row_off:row_off + grid_rows, col_off:col_off + grid_cols]
        kshift = key_pad[row_off:row_off + grid_rows, col_off:col_off + grid_cols]
        dprob = lax.optimization_barrier(jnp.sum(cot_heads * vshift, axis=-1))
        dscore = probs[index] * (dprob - delta)
        query_grad = query_grad + scale * dscore[..., None] * kshift
        key_acc = key_acc.at[row_off:row_off + grid_rows, col_off:col_off + grid_cols].add(scale * dscore[..., None] * query_heads)
        value_acc = value_acc.at[row_off:row_off + grid_rows, col_off:col_off + grid_cols].add(probs[index][..., None] * cot_heads)
    flat = (grid_rows, grid_cols, HEADS * HEAD_DIM)
    key_grad = key_acc[3:3 + grid_rows, 3:3 + grid_cols].reshape(flat)
    value_grad = value_acc[3:3 + grid_rows, 3:3 + grid_cols].reshape(flat)
    return (query_grad.reshape(flat), key_grad, value_grad)

def reference(queries, keys, values, cotangent):
    query_grad, key_grad, value_grad = jax.vmap(single_image)(queries, keys, values, cotangent)
    return (query_grad, key_grad, value_grad)
```

```python
import functools

import jax
import jax.numpy as jnp
from jax import lax
from jax.experimental import pallas as pl
from jax.experimental.pallas import tpu as pltpu
from jax.sharding import PartitionSpec as P

HEADS = 4
REACH = 3
FAR = 1000
NEG = -1e30
BF = jnp.bfloat16
F32 = jnp.float32


def pack_kernel(q_ref, k_ref, v_ref, c_ref, ha_ref, odd_ref, even_ref, corner_ref, split_ref):
    h = lax.axis_index("ha")
    p = lax.axis_index("wa") % 2
    row_in = jnp.where(h == 0, 5, 0)
    row_out = jnp.where(h == 0, 2, 3)
    row_all = jnp.where(h == 0, 2, 0)
    low_in, low_out = 0, 3
    high_in, high_out = 5, 2
    odd_in = jnp.where(p == 0, low_in, high_in)
    odd_out = jnp.where(p == 0, low_out, high_out)
    even_in = jnp.where(p == 0, high_in, low_in)
    even_out = jnp.where(p == 0, high_out, low_out)

    def rows(ref, image, first):
        start = pl.multiple_of(image * 64 + first * 8, 8)
        return ref[pl.ds(start, 24), :]

    fields = ((k_ref, True), (v_ref, True), (q_ref, False), (c_ref, False))
    for index, (ref, _) in enumerate(fields):
        for half in range(2):
            split_ref[2 * index + half] = ref[:, 128 * half : 128 * half + 128]

    def col(index, image, column, first, count):
        rows = pl.ds(image * 64 + first * 8 + column, count, stride=8)
        return jnp.concatenate([split_ref[2 * index + half, rows, :] for half in range(2)], axis=1)

    for image in range(2):
        at = image * 144
        for index, (ref, wide) in enumerate(fields):
            for part in range(2 if wide else 1):
                ha_ref[at : at + 24, :] = rows(ref, image, (row_in, row_out)[part])
                for j in range(3):
                    odd_ref[at + 8 * j : at + 8 * j + 8, :] = col(
                        index, image, (odd_in, odd_out)[part] + j, 0, 8
                    )
                    even_ref[at + 8 * j : at + 8 * j + 8, :] = col(
                        index, image, (even_in, even_out)[part] + j, 0, 8
                    )
                at += 24
        at = image * 90
        for index, (_, wide) in enumerate(fields):
            for j in range(3):
                corner_ref[at : at + 3, :] = col(index, image, odd_in + j, row_in, 3)
                at += 3
            if wide:
                for j in range(3):
                    corner_ref[at : at + 3, :] = col(index, image, odd_in + j, row_out, 3)
                    at += 3
                for j in range(3):
                    corner_ref[at : at + 6, :] = col(index, image, odd_out + j, row_all, 6)
                    at += 6


def third(i):
    return (i * 43) >> 7


def sixth(i):
    return (i * 43) >> 8


def segment_coords(h, p, alone, i):
    row_in = jnp.where(h == 0, 8, -3)
    row_out = jnp.where(h == 0, 11, -6)
    row_all = jnp.where(h == 0, 8, -6)
    even_in = jnp.where(p == 0, 8, -3)
    even_out = jnp.where(p == 0, 11, -6)
    even_all = jnp.where(p == 0, 8, -8)
    lost = jnp.where(alone, FAR, 0)
    odd_in = jnp.where(p == 0, -3, 8) + lost
    odd_out = jnp.where(p == 0, -6, 11) + lost
    hi, lo = i >> 3, i & 7
    inner = {
        "own": (hi, lo),
        "ha": (row_in + hi, lo),
        "even": (lo, even_in + hi),
        "odd": (lo, odd_in + hi),
        "deven": (row_in + hi, even_all + lo),
        "dodd": (row_in + (i - 3 * third(i)), odd_in + third(i)),
    }
    j = i - 9
    k = jnp.maximum(i - 9, 0)
    outer = {
        "ha": (row_out + hi, lo),
        "even": (lo, even_out + hi),
        "odd": (lo, odd_out + hi),
        "deven": (row_out + hi, even_all + lo),
        "dodd": (
            jnp.where(j < 0, row_out + (i - 3 * third(i)), row_all + (k - 6 * sixth(k))),
            jnp.where(j < 0, odd_in + third(i), odd_out + sixth(k)),
        ),
    }
    return inner, outer


def rounded(x):
    return x.astype(BF).astype(F32)


def swapped(x):
    return pltpu.roll(x, 64, 1)


def halves(x, parts):
    out = []
    for part in range(parts):
        top = rounded(x)
        out.append((top, swapped(top)))
        if part + 1 < parts:
            x = x - top
    return out


def side(low, a, b, odd):
    if odd:
        return jnp.where(low, b[1], a[0])
    return jnp.where(low, a[0], b[1])


def stacked(x, low, left, parts):
    out = []
    for pair in range(2):
        comps = halves(x[:, 128 * pair : 128 * pair + 128], parts)
        for odd in (False, True):
            if parts == 3:
                hi, mid, lo = comps
                if left:
                    a = side(low, hi, mid, odd).astype(BF)
                    pieces = [a, a, side(low, hi, lo, odd).astype(BF)]
                else:
                    pieces = [
                        side(low, hi, hi, odd).astype(BF),
                        side(low, mid, mid, odd).astype(BF),
                        side(low, lo, hi, odd).astype(BF),
                    ]
            else:
                hi, lo = comps
                if left:
                    a = side(low, hi, lo, odd).astype(BF)
                    pieces = [a, a]
                else:
                    pieces = [
                        side(low, hi, hi, odd).astype(BF),
                        side(low, lo, lo, odd).astype(BF),
                    ]
            out.append(jnp.concatenate(pieces, axis=1))
    return out


def dot_nt(a, b):
    return lax.dot_general(a, b, (((1,), (1,)), ((), ())), preferred_element_type=F32)


def dot_nn(a, b):
    return lax.dot_general(a, b, (((1,), (0,)), ((), ())), preferred_element_type=F32)


def two(x):
    hi = x.astype(BF)
    return hi, (x - hi.astype(F32)).astype(BF)


def heads_product(per_head, field, lane_head):
    left = jnp.concatenate(per_head, axis=0)
    left_hi, left_lo = two(left)
    right_hi, right_lo = field
    full = dot_nn(left_hi, right_hi) + (dot_nn(left_lo, right_hi) + dot_nn(left_hi, right_lo))
    out = full[0:64]
    for head in range(1, HEADS):
        out = jnp.where(lane_head == head, full[64 * head : 64 * head + 64], out)
    return out


def main_kernel(cols, q_ref, k_ref, v_ref, c_ref, ha_ref, even_ref, odd_ref, deven_ref, dodd_ref,
                dq_ref, dk_ref, dv_ref, bias_in_ref, bias_out_ref):
    h = lax.axis_index("ha")
    w = lax.axis_index("wa")
    p = w % 2
    alone = jnp.logical_or(w == 0, w == cols - 1)

    lane = lax.broadcasted_iota(jnp.int32, (8, 128), 1)
    token_r = jnp.full((8, 128), 3 * FAR, jnp.int32)
    token_c = jnp.full((8, 128), 3 * FAR, jnp.int32)
    for index, name in enumerate(("ha", "even", "odd", "deven", "dodd")):
        first = 24 * index
        r, c = segment_coords(h, p, alone, jnp.maximum(lane - first, 0))[0][name]
        inside = jnp.logical_and(lane >= first, lane < first + (9 if name == "dodd" else 24))
        token_r = jnp.where(inside, r, token_r)
        token_c = jnp.where(inside, c, token_c)
    own_r, own_c = lane >> 3, lane & 7

    def bias(r, c, tr, tc):
        near = jnp.logical_and(jnp.abs(r - tr) <= REACH, jnp.abs(c - tc) <= REACH)
        return jnp.where(near, 0.0, NEG).astype(F32)

    at_in, at_out = 0, 0
    for name, count_in, real_in, count_out, real_out in (
        ("own", 64, 64, 0, 0), ("ha", 24, 24, 24, 24), ("even", 24, 24, 24, 24),
        ("odd", 24, 24, 24, 24), ("deven", 24, 24, 24, 24), ("dodd", 16, 9, 32, 27),
    ):
        for group in range(max(count_in, count_out) // 8):
            i = lax.broadcasted_iota(jnp.int32, (8, 128), 0) + 8 * group
            inner, outer = segment_coords(h, p, alone, i)
            if 8 * group < count_in:
                r, c = inner[name]
                if 8 * group + 8 > real_in:
                    r = jnp.where(i < real_in, r, -FAR)
                bias_in_ref[at_in : at_in + 8, 0:128] = bias(r, c, token_r, token_c)
                bias_in_ref[at_in : at_in + 8, 128:256] = bias(r, c, own_r, own_c)
                at_in += 8
            if 8 * group < count_out:
                r, c = outer[name]
                if 8 * group + 8 > real_out:
                    r = jnp.where(i < real_out, r, -FAR)
                bias_out_ref[at_out : at_out + 8, :] = bias(r, c, token_r, token_c)
                at_out += 8

    low = lax.broadcasted_iota(jnp.int32, (1, 128), 1) < 64
    lane_head = lax.broadcasted_iota(jnp.int32, (1, 256), 1) >> 6
    halo = (ha_ref, even_ref, odd_ref, deven_ref)

    for image in range(2):
        here = slice(64 * image, 64 * image + 64)

        def key_side(ref, first, corner):
            a = 144 * image + first
            d = 90 * image + corner
            inner = [ref[here, :]] + [x[a : a + 24, :] for x in halo]
            inner += [dodd_ref[d : d + 9, :], jnp.zeros((7, 256), F32)]
            outer = [x[a + 24 : a + 48, :] for x in halo]
            outer += [dodd_ref[d + 9 : d + 36, :], jnp.zeros((5, 256), F32)]
            return jnp.concatenate(inner, axis=0), jnp.concatenate(outer, axis=0)

        def token_side(ref, first, corner):
            a = 144 * image + first
            d = 90 * image + corner
            parts = [x[a : a + 24, :] for x in halo]
            parts += [dodd_ref[d : d + 9, :], jnp.zeros((23, 256), F32), ref[here, :]]
            return jnp.concatenate(parts, axis=0)

        key_in, key_out = key_side(k_ref, 0, 0)
        value_in, value_out = key_side(v_ref, 48, 36)
        query = token_side(q_ref, 96, 72) * 0.125
        cot = token_side(c_ref, 120, 81)

        key_l = stacked(jnp.concatenate([key_in, key_out], axis=0), low, True, 3)
        value_l = stacked(jnp.concatenate([value_in, value_out], axis=0), low, True, 2)
        query_r = stacked(query, low, False, 3)
        cot_r = stacked(cot, low, False, 2)

        prob_rows, ds_rows, ds_cols = [], [], []
        for head in range(HEADS):
            s = dot_nt(key_l[head], query_r[head])
            dp = dot_nt(value_l[head], cot_r[head])
            s_halo = s[0:176, 0:128] + bias_in_ref[:, 0:128]
            s_own = s[0:176, 128:192] + bias_in_ref[:, 128:192]
            s_out = s[176:304, 0:128] + bias_out_ref[...]
            top_halo = jnp.maximum(
                jnp.maximum(
                    jnp.max(s_halo, axis=0, keepdims=True), jnp.max(s_out, axis=0, keepdims=True)
                ),
                -1e29,
            )
            top_own = jnp.max(s_own, axis=0, keepdims=True)
            e_halo = jnp.exp(s_halo - top_halo)
            e_out = jnp.exp(s_out - top_halo)
            e_own = jnp.exp(s_own - top_own)
            dp_halo, dp_own, dp_out = dp[0:176, 0:128], dp[0:176, 128:192], dp[176:304, 0:128]
            sum_halo = jnp.sum(e_halo, axis=0, keepdims=True) + jnp.sum(e_out, axis=0, keepdims=True)
            sum_own = jnp.sum(e_own, axis=0, keepdims=True)
            inv_halo = 1.0 / jnp.maximum(sum_halo, 1e-30)
            inv_own = 1.0 / sum_own
            delta_halo = inv_halo * (
                jnp.sum(e_halo * dp_halo, axis=0, keepdims=True)
                + jnp.sum(e_out * dp_out, axis=0, keepdims=True)
            )
            delta_own = inv_own * jnp.sum(e_own * dp_own, axis=0, keepdims=True)
            p_halo = e_halo[0:64] * inv_halo
            p_own = e_own * inv_own
            ds_halo = p_halo * (dp_halo[0:64] - delta_halo)
            ds_own = p_own * (dp_own - delta_own)
            prob_rows.append(jnp.concatenate([p_halo, p_own[0:64]], axis=1))
            ds_rows.append(jnp.concatenate([ds_halo, ds_own[0:64]], axis=1))
            ds_cols.append(ds_own.T)

        dv_ref[here, :] = heads_product(prob_rows, two(cot), lane_head)
        dk_ref[here, :] = heads_product(ds_rows, two(query), lane_head)
        dq_ref[here, :] = heads_product(ds_cols, two(key_in), lane_head) * 0.125


def per_device(queries, keys, values, cotangent):
    shape = queries.shape
    cols = lax.axis_size("wa")
    flat = [x.reshape(128, 256) for x in (queries, keys, values, cotangent)]
    message = jax.ShapeDtypeStruct((288, 256), F32)
    corner = jax.ShapeDtypeStruct((184, 256), F32)
    to_ha, to_odd, to_even, to_corner = pl.pallas_call(
        pack_kernel, out_shape=(message, message, message, corner),
        scratch_shapes=[pltpu.VMEM((8, 128, 128), F32)], name="pack",
    )(*flat)

    both = ("ha", "wa")
    ends = (0, cols - 1)
    partner = {i: (i + 1 if i % 2 else i - 1) for i in range(cols) if i not in ends}

    def number(row, col):
        return row * cols + col

    odd_pairs, corner_pairs = [], []
    for row in range(2):
        for col in range(cols):
            if col in ends:
                odd_pairs.append((number(row, col), number(1 - row, col)))
                corner_pairs.append((number(row, col), number(1 - row, col)))
            else:
                odd_pairs.append((number(row, col), number(row, partner[col])))
                corner_pairs.append((number(row, col), number(1 - row, partner[col])))
    even_pairs = [(i, i ^ 1) for i in range(cols)]

    from_ha = lax.ppermute(to_ha, "ha", [(0, 1), (1, 0)])
    from_odd = lax.ppermute(to_odd, both, odd_pairs)
    from_corner = lax.ppermute(to_corner, both, corner_pairs)
    from_even = lax.ppermute(to_even, "wa", even_pairs)
    from_deven = lax.ppermute(from_ha, "wa", even_pairs)

    out = jax.ShapeDtypeStruct((128, 256), F32)
    grads = pl.pallas_call(
        functools.partial(main_kernel, cols),
        out_shape=(out, out, out),
        scratch_shapes=[pltpu.VMEM((176, 256), F32), pltpu.VMEM((128, 128), F32)],
        compiler_params=pltpu.CompilerParams(vmem_limit_bytes=48 * 1024 * 1024),
        name="attend",
    )(*flat, from_ha, from_even, from_odd, from_deven, from_corner)
    return tuple(g.reshape(shape) for g in grads)


def solution(mesh):
    spec = P(None, "ha", "wa", None)
    return jax.shard_map(
        per_device,
        mesh=mesh,
        in_specs=(spec,) * 4,
        out_specs=(spec,) * 3,
        check_vma=False,
    )
```

```python
import functools

import jax
import jax.numpy as jnp
from jax import lax
from jax.experimental import pallas as pl
from jax.experimental.pallas import tpu as pltpu
from jax.sharding import PartitionSpec as P

HEADS = 4
REACH = 3
FAR = 1000
NEG = -1e30
BF = jnp.bfloat16
F32 = jnp.float32


def vmem(rows, columns=256, dtype=F32):
    return pltpu.VMEM((rows, columns), dtype)


def held(x):
    return pltpu.with_memory_space_constraint(x, pltpu.VMEM)


def slot_column(p, slot):
    turned = jnp.where(slot < 3, slot + 5, jnp.where(slot < 6, slot - 1, slot - 6))
    return jnp.where(p == 0, slot, turned)


def pack_kernel(q_ref, k_ref, v_ref, c_ref, corner_ref, rest_ref, odd_ref, even_ref,
                own_q_ref, own_k_ref, own_v_ref, own_c_ref, split_ref):
    h = lax.axis_index("ha")
    p = lax.axis_index("wa") % 2
    row_in = jnp.where(h == 0, 5, 0)
    row_out = jnp.where(h == 0, 2, 3)
    even_in = jnp.where(p == 0, 5, 0)
    even_out = jnp.where(p == 0, 2, 3)
    slots = [slot_column(p, slot) for slot in range(8)]

    fields = ((k_ref, own_k_ref, True), (v_ref, own_v_ref, True),
              (q_ref, own_q_ref, False), (c_ref, own_c_ref, False))
    for index, (ref, _, _) in enumerate(fields):
        for half in range(2):
            split_ref[2 * index + half] = ref[:, 128 * half : 128 * half + 128]

    def col(index, image, column, first, count):
        rows = pl.ds(image * 64 + first * 8 + column, count, stride=8)
        return jnp.concatenate([split_ref[2 * index + half, rows, :] for half in range(2)], axis=1)

    for image in range(2):
        at, rest = 90 * image, 54 * image
        for index, (_, _, wide) in enumerate(fields):
            pieces = [(row_in, slot) for slot in range(6 if wide else 3)]
            pieces += [(row_out, slot) for slot in range(6)] if wide else []
            for first, slot in pieces:
                corner_ref[at : at + 3, :] = col(index, image, slots[slot], first, 3)
                at += 3
            pieces = [(row_in, slot) for slot in ((6, 7) if wide else (3, 4, 5, 6, 7))]
            pieces += [(row_out, slot) for slot in (6, 7)] if wide else []
            for first, slot in pieces:
                rest_ref[rest : rest + 3, :] = col(index, image, slots[slot], first, 3)
                rest += 3
    for image in range(2):
        at = 144 * image
        for index, (_, own_ref, wide) in enumerate(fields):
            for slot in range(8):
                x = col(index, image, slots[slot], 0, 8)
                own_ref[64 * image + 8 * slot : 64 * image + 8 * slot + 8, :] = x
                if slot < (6 if wide else 3):
                    odd_ref[at + 8 * slot : at + 8 * slot + 8, :] = x
            for j in range(6 if wide else 3):
                even_ref[at + 8 * j : at + 8 * j + 8, :] = col(
                    index, image, even_in + j if j < 3 else even_out + j - 3, 0, 8
                )
            at += 48 if wide else 24


def third(i):
    return (i * 43) >> 7


class Places:
    def __init__(self, cols):
        h = lax.axis_index("ha")
        w = lax.axis_index("wa")
        self.p = p = w % 2
        lost = jnp.where(jnp.logical_or(w == 0, w == cols - 1), FAR, 0)
        self.row_in = jnp.where(h == 0, 8, -3)
        self.row_out = jnp.where(h == 0, 11, -6)
        self.even_in = jnp.where(p == 0, 8, -3)
        self.even_out = jnp.where(p == 0, 11, -6)
        self.even_all = jnp.where(p == 0, 8, -8)
        self.odd_in = jnp.where(p == 0, -3, 8) + lost
        self.odd_out = jnp.where(p == 0, -6, 11) + lost

    def own(self, i, slot=0):
        return i & 7, slot_column(self.p, slot + (i >> 3))

    def ha_in(self, i, slot=0):
        j = third(i)
        return self.row_in + (i - 3 * j), slot_column(self.p, slot + j)

    def ha_out(self, i):
        j = third(i)
        return self.row_out + (i - 3 * j), slot_column(self.p, j)

    def deven_in(self, i):
        j = third(i)
        return self.row_in + (i - 3 * j), self.even_all + slot_column(1 - self.p, j)

    def deven_out(self, i):
        j = third(i)
        return self.row_out + (i - 3 * j), self.even_all + slot_column(1 - self.p, j)

    def even_inner(self, i):
        return i & 7, self.even_in + (i >> 3)

    def even_outer(self, i):
        return i & 7, self.even_out + (i >> 3)

    def odd_inner(self, i):
        return i & 7, self.odd_in + (i >> 3)

    def odd_outer(self, i):
        return i & 7, self.odd_out + (i >> 3)

    def dodd_in(self, i):
        j = third(i)
        return self.row_in + (i - 3 * j), self.odd_in + j

    def dodd_out(self, i):
        near = i < 9
        k = jnp.where(near, i, i - 9)
        j = third(k)
        row = jnp.where(near, self.row_in, self.row_out) + (k - 3 * j)
        column = jnp.where(
            near, self.odd_out + j, jnp.where(j < 3, self.odd_in + j, self.odd_out + j - 3)
        )
        return row, column


def write_bias(bias_ref, key_segments, token_segments):
    lane = lax.broadcasted_iota(jnp.int32, (8, 128), 1)
    token_r = jnp.full((8, 128), 3 * FAR, jnp.int32)
    token_c = jnp.full((8, 128), 3 * FAR, jnp.int32)
    first = 0
    for place, real, count in token_segments:
        r, c = place(jnp.clip(lane - first, 0, real - 1))
        inside = jnp.logical_and(lane >= first, lane < first + real)
        token_r = jnp.where(inside, r, token_r)
        token_c = jnp.where(inside, c, token_c)
        first += count
    width = bias_ref.shape[1]
    at = 0
    for place, real, count in key_segments:
        for group in range(count // 8):
            i = lax.broadcasted_iota(jnp.int32, (8, 128), 0) + 8 * group
            r, c = place(jnp.minimum(i, real - 1))
            if 8 * group + 8 > real:
                r = jnp.where(i < real, r, -FAR)
            near = jnp.logical_and(jnp.abs(r - token_r) <= REACH, jnp.abs(c - token_c) <= REACH)
            bias_ref[at : at + 8, :] = jnp.where(near, 0.0, NEG).astype(F32)[:, 0:width]
            at += 8


def rounded(x):
    return x.astype(BF).astype(F32)


def halves(x, parts):
    out = []
    for part in range(parts):
        top = rounded(x)
        out.append((top, pltpu.roll(top, 64, 1)))
        if part + 1 < parts:
            x = x - top
    return out


def side(low, a, b, upper):
    if upper:
        return jnp.where(low, b[1], a[0])
    return jnp.where(low, a[0], b[1])


def stacked(x, left, parts):
    low = lax.broadcasted_iota(jnp.int32, (1, 128), 1) < 64
    out = []
    for pair in range(2):
        comps = halves(x[:, 128 * pair : 128 * pair + 128], parts)
        for upper in (False, True):
            if parts == 3:
                hi, mid, lo = comps
                if left:
                    a = side(low, hi, mid, upper).astype(BF)
                    pieces = [a, a, side(low, hi, lo, upper).astype(BF)]
                else:
                    pieces = [
                        side(low, hi, hi, upper).astype(BF),
                        side(low, mid, mid, upper).astype(BF),
                        side(low, lo, hi, upper).astype(BF),
                    ]
            else:
                hi, lo = comps
                if left:
                    a = side(low, hi, lo, upper).astype(BF)
                    pieces = [a, a]
                else:
                    pieces = [
                        side(low, hi, hi, upper).astype(BF),
                        side(low, lo, lo, upper).astype(BF),
                    ]
            out.append(jnp.concatenate(pieces, axis=1))
    return out


def dot_nt(a, b):
    return lax.dot_general(a, b, (((1,), (1,)), ((), ())), preferred_element_type=F32)


def dot_nn(a, b):
    return lax.dot_general(a, b, (((1,), (0,)), ((), ())), preferred_element_type=F32)


def two(x):
    hi = x.astype(BF)
    return hi, (x - hi.astype(F32)).astype(BF)


def heads_product(per_head, field):
    lane_head = lax.broadcasted_iota(jnp.int32, (1, 256), 1) >> 6
    rows = per_head[0].shape[0]
    left_hi, left_lo = two(jnp.concatenate(per_head, axis=0))
    right_hi, right_lo = two(field)
    full = dot_nn(left_hi, right_hi) + (dot_nn(left_lo, right_hi) + dot_nn(left_hi, right_lo))
    out = full[0:rows]
    for head in range(1, HEADS):
        out = jnp.where(lane_head == head, full[rows * head : rows * head + rows], out)
    return out


def attend(key, value, query, cot, bias_ref, own_tokens, own_keys, inner_keys):
    query = query * 0.125
    key_l, value_l = stacked(key, True, 3), stacked(value, True, 2)
    query_r, cot_r = stacked(query, False, 3), stacked(cot, False, 2)
    prob_rows, ds_rows, ds_cols = [], [], []
    for head in range(HEADS):
        s = dot_nt(key_l[head], query_r[head]) + bias_ref[...]
        dp = dot_nt(value_l[head], cot_r[head])
        top = jnp.maximum(jnp.max(s, axis=0, keepdims=True), -1e29)
        e = jnp.exp(s - top)
        inv = 1.0 / jnp.maximum(jnp.sum(e, axis=0, keepdims=True), 1e-30)
        delta = inv * jnp.sum(e * dp, axis=0, keepdims=True)
        probs = e[0:inner_keys] * inv
        ds = probs * (dp[0:inner_keys] - delta)
        prob_rows.append(probs[0:own_keys])
        ds_rows.append(ds[0:own_keys])
        ds_cols.append(ds[:, 0:own_tokens].T)
    return (
        heads_product(ds_cols, key[0:inner_keys]) * 0.125,
        heads_product(ds_rows, query),
        heads_product(prob_rows, cot),
    )


def rows(ref, first, count, pad=0):
    x = ref[first : first + count, :]
    return [x, jnp.zeros((pad, 256), F32)] if pad else [x]


CORNER = (0, 36, 72, 81)
REST = (0, 12, 24, 39)
SIDE = (0, 48, 96, 120)


def even_kernel(cols, own_q_ref, own_k_ref, own_v_ref, own_c_ref, corner_ref, rest_ref, even_ref, mate_corner_ref,
                mate_rest_ref, dq_ref, dk_ref, dv_ref, bias_ref):
    at = Places(cols)
    write_bias(
        bias_ref,
        ((at.own, 64, 64), (at.ha_in, 24, 24), (at.even_inner, 24, 24), (at.deven_in, 24, 24),
         (at.ha_out, 24, 24), (at.even_outer, 24, 24), (at.deven_out, 24, 24)),
        ((lambda i: at.own(i, 3), 40, 40), (lambda i: at.ha_in(i, 3), 15, 16), (at.even_inner, 24, 24),
         (at.deven_in, 24, 24)),
    )
    for image in range(2):

        def keys(own_ref, field):
            corner, rest, even = 90 * image + CORNER[field], 54 * image + REST[field], 144 * image + SIDE[field]
            out = rows(own_ref, 64 * image, 64)
            out += rows(corner_ref, corner, 18) + rows(rest_ref, rest, 6)
            out += rows(even_ref, even, 24)
            out += rows(mate_corner_ref, corner, 18) + rows(mate_rest_ref, rest, 6)
            out += rows(corner_ref, corner + 18, 18) + rows(rest_ref, rest + 6, 6)
            out += rows(even_ref, even + 24, 24)
            out += rows(mate_corner_ref, corner + 18, 18) + rows(mate_rest_ref, rest + 6, 6)
            return jnp.concatenate(out, axis=0)

        def tokens(own_ref, field):
            corner, rest, even = 90 * image + CORNER[field], 54 * image + REST[field], 144 * image + SIDE[field]
            out = rows(own_ref, 64 * image + 24, 40)
            out += rows(rest_ref, rest, 15, 1)
            out += rows(even_ref, even, 24)
            out += rows(mate_corner_ref, corner, 9) + rows(mate_rest_ref, rest, 15)
            return jnp.concatenate(out, axis=0)

        dq, dk, dv = attend(
            keys(own_k_ref, 0), keys(own_v_ref, 1), tokens(own_q_ref, 2), tokens(own_c_ref, 3), bias_ref, 40, 64, 136
        )
        dq_ref[40 * image : 40 * image + 40, :] = dq
        dk_ref[64 * image : 64 * image + 64, :] = dk
        dv_ref[64 * image : 64 * image + 64, :] = dv


def odd_kernel(cols, own_q_ref, own_k_ref, own_v_ref, own_c_ref, corner_ref, odd_ref, far_ref, even_dq_ref, even_dk_ref,
               even_dv_ref, dq_ref, dk_ref, dv_ref, bias_ref, split_ref):
    at = Places(cols)
    write_bias(
        bias_ref,
        ((at.own, 48, 48), (at.ha_in, 18, 24), (at.odd_inner, 24, 24), (at.dodd_in, 9, 16),
         (at.ha_out, 18, 24), (at.odd_outer, 24, 24), (at.dodd_out, 27, 32)),
        ((at.own, 24, 24), (at.ha_in, 9, 16), (at.odd_inner, 24, 24), (at.dodd_in, 9, 16)),
    )
    for image in range(2):

        def keys(own_ref, field):
            corner, odd = 90 * image + CORNER[field], 144 * image + SIDE[field]
            out = rows(own_ref, 64 * image, 48)
            out += rows(corner_ref, corner, 18, 6) + rows(odd_ref, odd, 24) + rows(far_ref, corner, 9, 7)
            out += rows(corner_ref, corner + 18, 18, 6) + rows(odd_ref, odd + 24, 24) + rows(far_ref, corner + 9, 27, 5)
            return jnp.concatenate(out, axis=0)

        def tokens(own_ref, field):
            corner, odd = 90 * image + CORNER[field], 144 * image + SIDE[field]
            out = rows(own_ref, 64 * image, 24)
            out += rows(corner_ref, corner, 9, 7) + rows(odd_ref, odd, 24) + rows(far_ref, corner, 9, 7)
            return jnp.concatenate(out, axis=0)

        dq, dk, dv = attend(
            keys(own_k_ref, 0), keys(own_v_ref, 1), tokens(own_q_ref, 2), tokens(own_c_ref, 3), bias_ref, 24, 48, 112
        )
        here = slice(64 * image, 64 * image + 64)
        none = jnp.zeros((16, 256), F32)
        results = (
            jnp.concatenate([dq, even_dq_ref[40 * image : 40 * image + 40, :]], axis=0),
            jnp.concatenate([dk, none], axis=0) + even_dk_ref[here, :],
            jnp.concatenate([dv, none], axis=0) + even_dv_ref[here, :],
        )
        for index, x in enumerate(results):
            for slot in range(8):
                where = pl.ds(64 * image + slot_column(at.p, slot), 8, stride=8)
                for half in range(2):
                    split_ref[2 * index + half, where, :] = x[8 * slot : 8 * slot + 8, 128 * half : 128 * half + 128]
    for index, ref in enumerate((dq_ref, dk_ref, dv_ref)):
        for half in range(2):
            ref[:, 128 * half : 128 * half + 128] = split_ref[2 * index + half]


def cost(micros):
    return pl.CostEstimate(flops=0, bytes_accessed=int(micros * 3e6), transcendentals=0)


def per_device(queries, keys, values, cotangent):
    shape = queries.shape
    cols = lax.axis_size("wa")
    flat = [x.reshape(128, 256) for x in (queries, keys, values, cotangent)]
    to_corner, to_rest, to_odd, to_even, *own = pl.pallas_call(
        pack_kernel,
        out_shape=(vmem(184), vmem(112), vmem(288), vmem(288)) + (vmem(128),) * 4,
        scratch_shapes=[pltpu.VMEM((8, 128, 128), F32)],
        name="pack",
    )(*flat)

    both = ("ha", "wa")
    ends = (0, cols - 1)
    partner = {i: (i + 1 if i % 2 else i - 1) for i in range(cols) if i not in ends}
    main_pairs, corner_pairs = [], []
    for row in range(2):
        for col in range(cols):
            here = row * cols + col
            if col in ends:
                main_pairs.append((here, row * cols + ends[1 - ends.index(col)]))
                corner_pairs.append((here, (1 - row) * cols + col))
            else:
                main_pairs.append((here, row * cols + partner[col]))
                corner_pairs.append((here, row * cols + partner[col]))
    even_pairs = [(i, i ^ 1) for i in range(cols)]
    across = [(0, 1), (1, 0)]

    corner = lax.ppermute(to_corner, "ha", across)
    odd = lax.ppermute(to_odd, both, main_pairs)
    rest = lax.ppermute(to_rest, "ha", across)
    even = lax.ppermute(to_even, "wa", even_pairs)
    far = lax.ppermute(corner, both, corner_pairs)
    mate_corner = lax.ppermute(corner, "wa", even_pairs)
    mate_rest = lax.ppermute(rest, "wa", even_pairs)

    even_part = pl.pallas_call(
        functools.partial(even_kernel, cols),
        out_shape=(vmem(80), vmem(128), vmem(128)),
        scratch_shapes=[pltpu.VMEM((208, 104), F32)],
        compiler_params=pltpu.CompilerParams(vmem_limit_bytes=32 * 1024 * 1024),
        name="even_set",
    )(*[held(x) for x in (*own, corner, rest, even, mate_corner, mate_rest)])
    out = jax.ShapeDtypeStruct((128, 256), F32)
    grads = pl.pallas_call(
        functools.partial(odd_kernel, cols),
        out_shape=(out, out, out),
        scratch_shapes=[pltpu.VMEM((192, 80), F32), pltpu.VMEM((6, 128, 128), F32)],
        compiler_params=pltpu.CompilerParams(vmem_limit_bytes=32 * 1024 * 1024),
        name="odd_set",
    )(*[held(x) for x in (*own, corner, odd, far, *even_part)])
    return tuple(g.reshape(shape) for g in grads)


def solution(mesh):
    spec = P(None, "ha", "wa", None)
    return jax.shard_map(
        per_device,
        mesh=mesh,
        in_specs=(spec,) * 4,
        out_specs=(spec,) * 3,
        check_vma=False,
    )
```

```python
import functools

import jax
import jax.numpy as jnp
from jax import lax
from jax.experimental import pallas as pl
from jax.experimental.pallas import tpu as pltpu
from jax.sharding import PartitionSpec as P

HEADS = 4
REACH = 3
FAR = 1000
NEG = -1e30
BF = jnp.bfloat16
F32 = jnp.float32


def vmem(rows, columns=256, dtype=F32):
    return pltpu.VMEM((rows, columns), dtype)


def held(x):
    return pltpu.with_memory_space_constraint(x, pltpu.VMEM)


def slot_column(p, slot):
    turned = jnp.where(slot < 3, slot + 5, jnp.where(slot < 6, slot - 1, slot - 6))
    return jnp.where(p == 0, slot, turned)


def pack_reader(split_ref):
    def col(index, image, column, first, count):
        rows = pl.ds(image * 64 + first * 8 + column, count, stride=8)
        return jnp.concatenate([split_ref[2 * index + half, rows, :] for half in range(2)], axis=1)

    return col


WIDE = (True, True, False, False)


def corner_kernel(k_ref, v_ref, q_ref, c_ref, corner_ref, split_ref):
    h = lax.axis_index("ha")
    p = lax.axis_index("wa") % 2
    row_in = jnp.where(h == 0, 5, 0)
    row_out = jnp.where(h == 0, 2, 3)
    col = pack_reader(split_ref)
    for index, ref in enumerate((k_ref, v_ref, q_ref, c_ref)):
        for half in range(2):
            split_ref[2 * index + half] = ref[:, 128 * half : 128 * half + 128]
    for image in range(2):
        at = 90 * image
        for index, wide in enumerate(WIDE):
            pieces = [(row_in, slot) for slot in range(6 if wide else 3)]
            pieces += [(row_out, slot) for slot in range(6)] if wide else []
            for first, slot in pieces:
                corner_ref[at : at + 3, :] = col(index, image, slot_column(p, slot), first, 3)
                at += 3


def pack_kernel(split_ref, rest_ref, odd_rest_ref, even_ref, own_k_ref, own_v_ref, own_q_ref, own_c_ref):
    h = lax.axis_index("ha")
    p = lax.axis_index("wa") % 2
    row_in = jnp.where(h == 0, 5, 0)
    row_out = jnp.where(h == 0, 2, 3)
    row_far = jnp.where(h == 0, 0, 6)
    row_rest = jnp.where(h == 0, 0, 3)
    even_in = jnp.where(p == 0, 5, 0)
    even_out = jnp.where(p == 0, 2, 3)
    slots = [slot_column(p, slot) for slot in range(8)]
    col = pack_reader(split_ref)
    for image in range(2):
        rest, odd_rest = 54 * image, 54 * image
        for index, wide in enumerate(WIDE):
            pieces = [(row_in, slot) for slot in ((6, 7) if wide else (3, 4, 5, 6, 7))]
            pieces += [(row_out, slot) for slot in (6, 7)] if wide else []
            for first, slot in pieces:
                rest_ref[rest : rest + 3, :] = col(index, image, slots[slot], first, 3)
                rest += 3
            for slot in range(6 if wide else 3):
                first, count = (row_far, 2) if wide else (row_rest, 5)
                odd_rest_ref[odd_rest : odd_rest + count, :] = col(index, image, slots[slot], first, count)
                odd_rest += count
    for image in range(2):
        at = 144 * image
        for index, (own_ref, wide) in enumerate(zip((own_k_ref, own_v_ref, own_q_ref, own_c_ref), WIDE)):
            for slot in range(8):
                own_ref[64 * image + 8 * slot : 64 * image + 8 * slot + 8, :] = col(index, image, slots[slot], 0, 8)
            for j in range(6 if wide else 3):
                even_ref[at + 8 * j : at + 8 * j + 8, :] = col(
                    index, image, even_in + j if j < 3 else even_out + j - 3, 0, 8
                )
            at += 48 if wide else 24


def third(i):
    return (i * 43) >> 7


class Places:
    def __init__(self, cols):
        h = lax.axis_index("ha")
        w = lax.axis_index("wa")
        self.p = p = w % 2
        lost = jnp.where(jnp.logical_or(w == 0, w == cols - 1), FAR, 0)
        self.row_in = jnp.where(h == 0, 8, -3)
        self.row_out = jnp.where(h == 0, 11, -6)
        self.even_in = jnp.where(p == 0, 8, -3)
        self.even_out = jnp.where(p == 0, 11, -6)
        self.even_all = jnp.where(p == 0, 8, -8)
        self.row_near = jnp.where(h == 0, 5, 0)
        self.row_next = jnp.where(h == 0, 2, 3)
        self.row_far = jnp.where(h == 0, 0, 6)
        self.row_rest = jnp.where(h == 0, 0, 3)
        self.odd_in = jnp.where(p == 0, -3, 8) + lost
        self.odd_out = jnp.where(p == 0, -6, 11) + lost

    def own(self, i, slot=0):
        return i & 7, slot_column(self.p, slot + (i >> 3))

    def ha_in(self, i, slot=0):
        j = third(i)
        return self.row_in + (i - 3 * j), slot_column(self.p, slot + j)

    def ha_out(self, i):
        j = third(i)
        return self.row_out + (i - 3 * j), slot_column(self.p, j)

    def deven_in(self, i):
        j = third(i)
        return self.row_in + (i - 3 * j), self.even_all + slot_column(1 - self.p, j)

    def deven_out(self, i):
        j = third(i)
        return self.row_out + (i - 3 * j), self.even_all + slot_column(1 - self.p, j)

    def even_inner(self, i):
        return i & 7, self.even_in + (i >> 3)

    def even_outer(self, i):
        return i & 7, self.even_out + (i >> 3)

    def odd_keys(self, i):
        k = jnp.where(i < 9, i, jnp.where(i < 18, i - 9, 0))
        j = third(k)
        row = jnp.where(i < 9, self.row_near, self.row_next) + (k - 3 * j)
        m = jnp.maximum(i - 18, 0)
        last = i >= 18
        return jnp.where(last, self.row_far + (m & 1), row), jnp.where(last, m >> 1, j)

    def odd_inner(self, i):
        row, j = self.odd_keys(i)
        return row, self.odd_in + j

    def odd_outer(self, i):
        row, j = self.odd_keys(i)
        return row, self.odd_out + j

    def odd_tokens(self, i):
        j = third(i)
        m = jnp.maximum(i - 9, 0)
        fifth = (m * 13) >> 6
        near = i < 9
        return (
            jnp.where(near, self.row_near + (i - 3 * j), self.row_rest + (m - 5 * fifth)),
            self.odd_in + jnp.where(near, j, fifth),
        )

    def dodd_in(self, i):
        j = third(i)
        return self.row_in + (i - 3 * j), self.odd_in + j

    def dodd_out(self, i):
        near = i < 9
        k = jnp.where(near, i, i - 9)
        j = third(k)
        row = jnp.where(near, self.row_in, self.row_out) + (k - 3 * j)
        column = jnp.where(
            near, self.odd_out + j, jnp.where(j < 3, self.odd_in + j, self.odd_out + j - 3)
        )
        return row, column


def write_bias(bias_ref, key_segments, token_segments):
    lane = lax.broadcasted_iota(jnp.int32, (8, 128), 1)
    token_r = jnp.full((8, 128), 3 * FAR, jnp.int32)
    token_c = jnp.full((8, 128), 3 * FAR, jnp.int32)
    first = 0
    for place, real, count in token_segments:
        r, c = place(jnp.clip(lane - first, 0, real - 1))
        inside = jnp.logical_and(lane >= first, lane < first + real)
        token_r = jnp.where(inside, r, token_r)
        token_c = jnp.where(inside, c, token_c)
        first += count
    width = bias_ref.shape[1]
    at = 0
    for place, real, count in key_segments:
        for group in range(count // 8):
            i = lax.broadcasted_iota(jnp.int32, (8, 128), 0) + 8 * group
            r, c = place(jnp.minimum(i, real - 1))
            if 8 * group + 8 > real:
                r = jnp.where(i < real, r, -FAR)
            near = jnp.logical_and(jnp.abs(r - token_r) <= REACH, jnp.abs(c - token_c) <= REACH)
            bias_ref[at : at + 8, :] = jnp.where(near, 0.0, NEG).astype(F32)[:, 0:width]
            at += 8


def rounded(x):
    return x.astype(BF).astype(F32)


def halves(x, parts):
    out = []
    for part in range(parts):
        top = rounded(x)
        out.append((top, pltpu.roll(top, 64, 1)))
        if part + 1 < parts:
            x = x - top
    return out


def side(low, a, b, upper):
    if upper:
        return jnp.where(low, b[1], a[0])
    return jnp.where(low, a[0], b[1])


def stacked(x, left, parts):
    low = lax.broadcasted_iota(jnp.int32, (1, 128), 1) < 64
    out = []
    for pair in range(2):
        comps = halves(x[:, 128 * pair : 128 * pair + 128], parts)
        for upper in (False, True):
            if parts == 3:
                hi, mid, lo = comps
                if left:
                    a = side(low, hi, mid, upper).astype(BF)
                    pieces = [a, a, side(low, hi, lo, upper).astype(BF)]
                else:
                    pieces = [
                        side(low, hi, hi, upper).astype(BF),
                        side(low, mid, mid, upper).astype(BF),
                        side(low, lo, hi, upper).astype(BF),
                    ]
            else:
                hi, lo = comps
                if left:
                    a = side(low, hi, lo, upper).astype(BF)
                    pieces = [a, a]
                else:
                    pieces = [
                        side(low, hi, hi, upper).astype(BF),
                        side(low, lo, lo, upper).astype(BF),
                    ]
            whole = jnp.concatenate(pieces, axis=1)
            if not left:
                whole = jnp.concatenate([whole, jnp.zeros((128 - whole.shape[0], whole.shape[1]), BF)], axis=0)
            out.append(whole)
    return out


def dot_nt(a, b):
    return lax.dot_general(a, b, (((1,), (1,)), ((), ())), preferred_element_type=F32)


def dot_nn(a, b):
    return lax.dot_general(a, b, (((1,), (0,)), ((), ())), preferred_element_type=F32)


def two(x):
    hi = x.astype(BF)
    return hi, (x - hi.astype(F32)).astype(BF)


def heads_product(per_head, field):
    low = lax.broadcasted_iota(jnp.int32, (1, 128), 1) < 64
    rows, depth = per_head[0].shape
    hi, lo = two(field)
    if hi.shape[0] < depth:
        more = jnp.zeros((depth - hi.shape[0], 256), BF)
        hi, lo = jnp.concatenate([hi, more], axis=0), jnp.concatenate([lo, more], axis=0)
    out = []
    for pair in range(2):
        lanes = slice(128 * pair, 128 * pair + 128)
        left_hi, left_lo = two(jnp.concatenate(per_head[2 * pair : 2 * pair + 2], axis=0))
        both = jnp.concatenate([hi[:, lanes], lo[:, lanes]], axis=1)
        if depth == 128:
            below = jnp.concatenate([hi[:, lanes], jnp.zeros((depth, 128), BF)], axis=1)
            full = dot_nn(jnp.concatenate([left_hi, left_lo], axis=1), jnp.concatenate([both, below], axis=0))
            full = full[:, 0:128] + full[:, 128:256]
        else:
            full = dot_nn(left_hi, both)
            full = full[:, 0:128] + (full[:, 128:256] + dot_nn(left_lo, hi[:, lanes]))
        out.append(jnp.where(low, full[0:rows], full[rows : 2 * rows]))
    return jnp.concatenate(out, axis=1)


def attend(work, bias_ref, own_tokens, own_keys, inner):
    scores, dprobs = [], []
    for key_l, value_l, query_r, cot_r, _, _, _ in work:
        for head in range(HEADS):
            scores.append(dot_nt(key_l[head], query_r[head]) + bias_ref[...])
            dprobs.append(dot_nt(value_l[head], cot_r[head]))
    prob_rows, ds_rows, ds_cols = [], [], []
    for s, dp in zip(scores, dprobs):
        top = jnp.maximum(jnp.max(s, axis=0, keepdims=True), -1e29)
        e = jnp.exp(s - top)
        inv = 1.0 / jnp.maximum(jnp.sum(e, axis=0, keepdims=True), 1e-30)
        delta = inv * jnp.sum(e * dp, axis=0, keepdims=True)
        prob_rows.append(e[0:own_keys] * inv)
        ds = [e[part] * inv * (dp[part] - delta) for part in inner]
        ds_rows.append(ds[0][0:own_keys])
        ds = jnp.concatenate(ds, axis=0) if len(ds) > 1 else ds[0]
        ds_cols.append(ds[:, 0:own_tokens].T)
    out = []
    for image, (_, _, _, _, key, query, cot) in enumerate(work):
        here = slice(HEADS * image, HEADS * image + HEADS)
        out.append((
            heads_product(ds_cols[here], key) * 0.125,
            heads_product(ds_rows[here], query),
            heads_product(prob_rows[here], cot),
        ))
    return out


def rows(ref, first, count, pad=0):
    x = ref[first : first + count, :]
    return [x, jnp.zeros((pad, 256), F32)] if pad else [x]


CORNER = (0, 36, 72, 81)
REST = (0, 12, 24, 39)
SIDE = (0, 48, 96, 120)


def even_kernel(cols, own_q_ref, own_k_ref, own_v_ref, own_c_ref, corner_ref, rest_ref, even_ref, mate_ref, dq_ref, dk_ref, dv_ref, bias_ref):
    at = Places(cols)
    write_bias(
        bias_ref,
        ((at.own, 64, 64), (at.ha_in, 24, 24), (at.even_inner, 24, 24), (at.deven_in, 24, 24),
         (at.ha_out, 24, 24), (at.even_outer, 24, 24), (at.deven_out, 24, 24)),
        ((lambda i: at.own(i, 3), 40, 40), (lambda i: at.ha_in(i, 3), 15, 16), (at.even_inner, 24, 24),
         (at.deven_in, 24, 24)),
    )
    work = []
    for image in range(2):

        def keys(own_ref, field):
            corner, rest, even = 90 * image + CORNER[field], 54 * image + REST[field], 144 * image + SIDE[field]
            out = rows(own_ref, 64 * image, 64)
            out += rows(corner_ref, corner, 18) + rows(rest_ref, rest, 6)
            out += rows(even_ref, even, 24)
            out += rows(mate_ref, corner, 18) + rows(mate_ref, 184 + rest, 6)
            out += rows(corner_ref, corner + 18, 18) + rows(rest_ref, rest + 6, 6)
            out += rows(even_ref, even + 24, 24)
            out += rows(mate_ref, corner + 18, 18) + rows(mate_ref, 184 + rest + 6, 6)
            return jnp.concatenate(out, axis=0)

        def tokens(own_ref, field):
            corner, rest, even = 90 * image + CORNER[field], 54 * image + REST[field], 144 * image + SIDE[field]
            out = rows(own_ref, 64 * image + 24, 40)
            out += rows(rest_ref, rest, 15, 1)
            out += rows(even_ref, even, 24)
            out += rows(mate_ref, corner, 9) + rows(mate_ref, 184 + rest, 15, 8)
            return jnp.concatenate(out, axis=0)

        key, query, cot = keys(own_k_ref, 0), tokens(own_q_ref, 2) * 0.125, tokens(own_c_ref, 3)
        work.append((
            stacked(key, True, 3), stacked(keys(own_v_ref, 1), True, 2), stacked(query, False, 3), stacked(cot, False, 2),
            key[0:136], query, cot,
        ))
    for image, (dq, dk, dv) in enumerate(attend(work, bias_ref, 40, 64, (slice(0, 136),))):
        dq_ref[40 * image : 40 * image + 40, :] = dq
        dk_ref[64 * image : 64 * image + 64, :] = dk
        dv_ref[64 * image : 64 * image + 64, :] = dv


def early_tokens(image, own_ref, corner_ref, odd_ref, odd_rest_ref, field):
    corner, rest = 90 * image + CORNER[field], 54 * image + REST[field]
    out = rows(own_ref, 64 * image, 24)
    out += rows(corner_ref, corner, 9, 7)
    out += rows(odd_ref, corner, 9) + rows(odd_rest_ref, rest, 15)
    return jnp.concatenate(out, axis=0)


def sort_kernel(cols, first_ref, second_ref, rest_ref, ha_ref, odd_ref, mate_ref):
    turned = by_row(lax.axis_index("wa"), cols)
    first, second = first_ref[...], second_ref[...]
    ha = jnp.where(turned, second, first)
    ha_ref[...] = ha
    odd_ref[...] = jnp.where(turned, first, second)
    mate_ref[0:184, :] = ha
    mate_ref[184:296, :] = rest_ref[...]


def release_kernel(message_ref, gate_ref, out_ref):
    out_ref[...] = message_ref[...]


def by_row(w, cols):
    return jnp.logical_and(((w + 1) >> 1) % 2 == 0, jnp.logical_and(w > 0, w < cols - 1))


def odd_kernel(cols, own_q_ref, own_k_ref, own_v_ref, own_c_ref, corner_ref, odd_ref, odd_rest_ref, far_ref, even_dq_ref,
               even_dk_ref, even_dv_ref, dq_ref, dk_ref, dv_ref, bias_ref, split_ref):
    at = Places(cols)
    p = at.p
    write_bias(
        bias_ref,
        ((at.own, 48, 48), (at.ha_in, 18, 24), (at.odd_inner, 24, 24), (at.ha_out, 18, 24), (at.odd_outer, 24, 24),
         (at.dodd_in, 9, 16), (at.dodd_out, 27, 32)),
        ((at.own, 24, 24), (at.ha_in, 9, 16), (at.odd_tokens, 24, 24), (at.dodd_in, 9, 16)),
    )
    work = []
    for image in range(2):

        def keys(own_ref, field):
            corner, rest = 90 * image + CORNER[field], 54 * image + REST[field]
            out = rows(own_ref, 64 * image, 48)
            out += rows(corner_ref, corner, 18, 6)
            out += rows(odd_ref, corner, 9) + rows(odd_ref, corner + 18, 9) + rows(odd_rest_ref, rest, 6)
            out += rows(corner_ref, corner + 18, 18, 6)
            out += rows(odd_ref, corner + 9, 9) + rows(odd_ref, corner + 27, 9) + rows(odd_rest_ref, rest + 6, 6)
            out += rows(far_ref, corner, 9, 7) + rows(far_ref, corner + 9, 27, 5)
            return jnp.concatenate(out, axis=0)

        def tokens(own_ref, field):
            corner, rest = 90 * image + CORNER[field], 54 * image + REST[field]
            out = rows(own_ref, 64 * image, 24)
            out += rows(corner_ref, corner, 9, 7)
            out += rows(odd_ref, corner, 9) + rows(odd_rest_ref, rest, 15)
            out += rows(far_ref, corner, 9, 7)
            return jnp.concatenate(out, axis=0)

        key, query, cot = keys(own_k_ref, 0), tokens(own_q_ref, 2) * 0.125, tokens(own_c_ref, 3)
        work.append((
            stacked(key, True, 3), stacked(keys(own_v_ref, 1), True, 2), stacked(query, False, 3), stacked(cot, False, 2),
            jnp.concatenate([key[0:96], key[144:160]], axis=0), query, cot,
        ))
    parts = attend(work, bias_ref, 24, 48, (slice(0, 96), slice(144, 160)))
    for image, (dq, dk, dv) in enumerate(parts):
        here = slice(64 * image, 64 * image + 64)
        none = jnp.zeros((16, 256), F32)
        results = (
            jnp.concatenate([dq, even_dq_ref[40 * image : 40 * image + 40, :]], axis=0),
            jnp.concatenate([dk, none], axis=0) + even_dk_ref[here, :],
            jnp.concatenate([dv, none], axis=0) + even_dv_ref[here, :],
        )
        for index, x in enumerate(results):
            for slot in range(8):
                where = pl.ds(64 * image + slot_column(p, slot), 8, stride=8)
                for half in range(2):
                    split_ref[2 * index + half, where, :] = x[8 * slot : 8 * slot + 8, 128 * half : 128 * half + 128]
    for index, ref in enumerate((dq_ref, dk_ref, dv_ref)):
        for half in range(2):
            ref[:, 128 * half : 128 * half + 128] = split_ref[2 * index + half]


PREP_US = 1
FAR_US = 2
EVEN_US = 0


def cost(micros):
    return pl.CostEstimate(flops=int(micros * 1e9), bytes_accessed=int(micros * 3e6), transcendentals=0)


def per_device(queries, keys, values, cotangent):
    shape = queries.shape
    cols = lax.axis_size("wa")
    flat = [x.reshape(128, 256) for x in (queries, keys, values, cotangent)]
    to_corner, split = pl.pallas_call(
        corner_kernel, out_shape=(vmem(184), pltpu.VMEM((8, 128, 128), F32)), name="corner"
    )(flat[1], flat[2], flat[0], flat[3])
    to_rest, to_odd_rest, to_even, own_k, own_v, own_q, own_c = pl.pallas_call(
        pack_kernel, out_shape=(vmem(112), vmem(112), vmem(288)) + (vmem(128),) * 4, name="pack"
    )(held(split))
    own = (own_q, own_k, own_v, own_c)

    both = ("ha", "wa")
    ends = (0, cols - 1)
    partner = {i: (i + 1 if i % 2 else i - 1) for i in range(cols) if i not in ends}
    first_pairs, second_pairs, far_pairs, odd_pairs = [], [], [], []
    for row in range(2):
        for col in range(cols):
            here, mate = row * cols + col, (1 - row) * cols + col
            beside = mate if col in ends else row * cols + partner[col]
            turned = (col + 1) // 2 % 2 == 0
            first_pairs.append((here, beside if turned else mate))
            far_pairs.append((here, mate if turned else beside))
            second_pairs.append((here, here if col in ends else mate if turned else beside))
            odd_pairs.append((here, beside))
    even_pairs = [(i, i ^ 1) for i in range(cols)]
    across = [(0, 1), (1, 0)]

    first = lax.ppermute(to_corner, both, first_pairs)
    second = lax.ppermute(to_corner, both, second_pairs)
    rest = lax.ppermute(to_rest, "ha", across)
    odd_rest = lax.ppermute(to_odd_rest, both, odd_pairs)
    to_even = pl.pallas_call(release_kernel, out_shape=vmem(288), name="release")(held(to_even), held(first))
    even = lax.ppermute(to_even, "wa", even_pairs)
    far = lax.ppermute(first, both, far_pairs)
    corner, odd, to_mate = pl.pallas_call(
        functools.partial(sort_kernel, cols), out_shape=(vmem(184), vmem(184), vmem(296)), name="sort"
    )(*[held(x) for x in (first, second, rest)])
    mate = lax.ppermute(to_mate, "wa", even_pairs)

    if PREP_US:
        odd_rest = pl.pallas_call(
            release_kernel, out_shape=vmem(112), cost_estimate=cost(PREP_US), name="arrive"
        )(held(odd_rest), held(first))
    if FAR_US:
        far = pl.pallas_call(
            release_kernel, out_shape=vmem(184), cost_estimate=cost(FAR_US), name="arrive_far"
        )(held(far), held(first))
    even_part = pl.pallas_call(
        functools.partial(even_kernel, cols),
        out_shape=(vmem(80), vmem(128), vmem(128)),
        scratch_shapes=[pltpu.VMEM((208, 128), F32)],
        compiler_params=pltpu.CompilerParams(vmem_limit_bytes=16 * 1024 * 1024),
        cost_estimate=cost(EVEN_US),
        name="even_set",
    )(*[held(x) for x in (*own, corner, rest, even, mate)])
    out = jax.ShapeDtypeStruct((128, 256), F32)
    grads = pl.pallas_call(
        functools.partial(odd_kernel, cols),
        out_shape=(out, out, out),
        scratch_shapes=[pltpu.VMEM((192, 128), F32), pltpu.VMEM((6, 128, 128), F32)],
        compiler_params=pltpu.CompilerParams(vmem_limit_bytes=16 * 1024 * 1024),
        name="odd_set",
    )(*[held(x) for x in (*own, corner, odd, odd_rest, far, *even_part)])
    return tuple(g.reshape(shape) for g in grads)


def solution(mesh):
    spec = P(None, "ha", "wa", None)
    return jax.shard_map(
        per_device,
        mesh=mesh,
        in_specs=(spec,) * 4,
        out_specs=(spec,) * 3,
        check_vma=False,
    )
```

```python
import functools

import jax
import jax.numpy as jnp
from jax import lax
from jax.experimental import pallas as pl
from jax.experimental.pallas import tpu as pltpu
from jax.sharding import PartitionSpec as P

HEADS = 4
REACH = 3
FAR = 1000
NEG = -1e30
BF = jnp.bfloat16
F32 = jnp.float32


def vmem(rows, columns=256, dtype=F32):
    return pltpu.VMEM((rows, columns), dtype)


def held(x):
    return pltpu.with_memory_space_constraint(x, pltpu.VMEM)


def slot_column(p, slot):
    turned = jnp.where(slot < 3, slot + 5, jnp.where(slot < 6, slot - 1, slot - 6))
    return jnp.where(p == 0, slot, turned)


def pack_reader(split_ref):
    def col(index, image, column, first, count):
        rows = pl.ds(image * 64 + first * 8 + column, count, stride=8)
        return jnp.concatenate([split_ref[2 * index + half, rows, :] for half in range(2)], axis=1)

    return col


WIDE = (True, True, False, False)


def corner_kernel(k_ref, v_ref, q_ref, c_ref, corner_ref, split_ref):
    h = lax.axis_index("ha")
    p = lax.axis_index("wa") % 2
    row_in = jnp.where(h == 0, 5, 0)
    row_out = jnp.where(h == 0, 2, 3)
    col = pack_reader(split_ref)
    for index, ref in enumerate((k_ref, v_ref, q_ref, c_ref)):
        for half in range(2):
            split_ref[2 * index + half] = ref[:, 128 * half : 128 * half + 128]
    for image in range(2):
        at = 90 * image
        for index, wide in enumerate(WIDE):
            pieces = [(row_in, slot) for slot in range(6 if wide else 3)]
            pieces += [(row_out, slot) for slot in range(6)] if wide else []
            for first, slot in pieces:
                corner_ref[at : at + 3, :] = col(index, image, slot_column(p, slot), first, 3)
                at += 3


def pack_kernel(split_ref, rest_ref, odd_rest_ref, even_ref, own_k_ref, own_v_ref, own_q_ref, own_c_ref):
    h = lax.axis_index("ha")
    p = lax.axis_index("wa") % 2
    row_in = jnp.where(h == 0, 5, 0)
    row_out = jnp.where(h == 0, 2, 3)
    row_far = jnp.where(h == 0, 0, 6)
    row_rest = jnp.where(h == 0, 0, 3)
    even_in = jnp.where(p == 0, 5, 0)
    even_out = jnp.where(p == 0, 2, 3)
    slots = [slot_column(p, slot) for slot in range(8)]
    col = pack_reader(split_ref)
    for image in range(2):
        rest, odd_rest = 54 * image, 54 * image
        for index, wide in enumerate(WIDE):
            pieces = [(row_in, slot) for slot in ((6, 7) if wide else (3, 4, 5, 6, 7))]
            pieces += [(row_out, slot) for slot in (6, 7)] if wide else []
            for first, slot in pieces:
                rest_ref[rest : rest + 3, :] = col(index, image, slots[slot], first, 3)
                rest += 3
            for slot in range(6 if wide else 3):
                first, count = (row_far, 2) if wide else (row_rest, 5)
                odd_rest_ref[odd_rest : odd_rest + count, :] = col(index, image, slots[slot], first, count)
                odd_rest += count
    for image in range(2):
        at = 144 * image
        for index, (own_ref, wide) in enumerate(zip((own_k_ref, own_v_ref, own_q_ref, own_c_ref), WIDE)):
            for slot in range(8):
                own_ref[64 * image + 8 * slot : 64 * image + 8 * slot + 8, :] = col(index, image, slots[slot], 0, 8)
            for j in range(6 if wide else 3):
                even_ref[at + 8 * j : at + 8 * j + 8, :] = col(
                    index, image, even_in + j if j < 3 else even_out + j - 3, 0, 8
                )
            at += 48 if wide else 24


def third(i):
    return (i * 43) >> 7


class Places:
    def __init__(self, cols):
        h = lax.axis_index("ha")
        w = lax.axis_index("wa")
        self.p = p = w % 2
        lost = jnp.where(jnp.logical_or(w == 0, w == cols - 1), FAR, 0)
        self.row_in = jnp.where(h == 0, 8, -3)
        self.row_out = jnp.where(h == 0, 11, -6)
        self.even_in = jnp.where(p == 0, 8, -3)
        self.even_out = jnp.where(p == 0, 11, -6)
        self.even_all = jnp.where(p == 0, 8, -8)
        self.row_near = jnp.where(h == 0, 5, 0)
        self.row_next = jnp.where(h == 0, 2, 3)
        self.row_far = jnp.where(h == 0, 0, 6)
        self.row_rest = jnp.where(h == 0, 0, 3)
        self.odd_in = jnp.where(p == 0, -3, 8) + lost
        self.odd_out = jnp.where(p == 0, -6, 11) + lost

    def own(self, i, slot=0):
        return i & 7, slot_column(self.p, slot + (i >> 3))

    def ha_in(self, i, slot=0):
        j = third(i)
        return self.row_in + (i - 3 * j), slot_column(self.p, slot + j)

    def ha_out(self, i):
        j = third(i)
        return self.row_out + (i - 3 * j), slot_column(self.p, j)

    def deven_in(self, i):
        j = third(i)
        return self.row_in + (i - 3 * j), self.even_all + slot_column(1 - self.p, j)

    def deven_out(self, i):
        j = third(i)
        return self.row_out + (i - 3 * j), self.even_all + slot_column(1 - self.p, j)

    def even_inner(self, i):
        return i & 7, self.even_in + (i >> 3)

    def even_outer(self, i):
        return i & 7, self.even_out + (i >> 3)

    def odd_keys(self, i):
        k = jnp.where(i < 9, i, jnp.where(i < 18, i - 9, 0))
        j = third(k)
        row = jnp.where(i < 9, self.row_near, self.row_next) + (k - 3 * j)
        m = jnp.maximum(i - 18, 0)
        last = i >= 18
        return jnp.where(last, self.row_far + (m & 1), row), jnp.where(last, m >> 1, j)

    def odd_inner(self, i):
        row, j = self.odd_keys(i)
        return row, self.odd_in + j

    def odd_outer(self, i):
        row, j = self.odd_keys(i)
        return row, self.odd_out + j

    def odd_tokens(self, i):
        j = third(i)
        m = jnp.maximum(i - 9, 0)
        fifth = (m * 13) >> 6
        near = i < 9
        return (
            jnp.where(near, self.row_near + (i - 3 * j), self.row_rest + (m - 5 * fifth)),
            self.odd_in + jnp.where(near, j, fifth),
        )

    def dodd_in(self, i):
        j = third(i)
        return self.row_in + (i - 3 * j), self.odd_in + j

    def dodd_out(self, i):
        near = i < 9
        k = jnp.where(near, i, i - 9)
        j = third(k)
        row = jnp.where(near, self.row_in, self.row_out) + (k - 3 * j)
        column = jnp.where(
            near, self.odd_out + j, jnp.where(j < 3, self.odd_in + j, self.odd_out + j - 3)
        )
        return row, column


def write_bias(bias_ref, key_segments, token_segments):
    lane = lax.broadcasted_iota(jnp.int32, (8, 128), 1)
    token_r = jnp.full((8, 128), 3 * FAR, jnp.int32)
    token_c = jnp.full((8, 128), 3 * FAR, jnp.int32)
    first = 0
    for place, real, count in token_segments:
        if place is None:
            first += count
            continue
        r, c = place(jnp.clip(lane - first, 0, real - 1))
        inside = jnp.logical_and(lane >= first, lane < first + real)
        token_r = jnp.where(inside, r, token_r)
        token_c = jnp.where(inside, c, token_c)
        first += count
    width = bias_ref.shape[1]
    at = 0
    for place, real, count in key_segments:
        for group in range(count // 8):
            i = lax.broadcasted_iota(jnp.int32, (8, 128), 0) + 8 * group
            r, c = place(jnp.minimum(i, real - 1))
            if 8 * group + 8 > real:
                r = jnp.where(i < real, r, -FAR)
            near = jnp.logical_and(jnp.abs(r - token_r) <= REACH, jnp.abs(c - token_c) <= REACH)
            bias_ref[at : at + 8, :] = jnp.where(near, 0.0, NEG).astype(F32)[:, 0:width]
            at += 8


def rounded(x):
    return x.astype(BF).astype(F32)


def halves(x, parts):
    out = []
    for part in range(parts):
        top = rounded(x)
        out.append((top, pltpu.roll(top, 64, 1)))
        if part + 1 < parts:
            x = x - top
    return out


def side(low, a, b, upper):
    if upper:
        return jnp.where(low, b[1], a[0])
    return jnp.where(low, a[0], b[1])


def stacked(x, left, parts):
    low = lax.broadcasted_iota(jnp.int32, (1, 128), 1) < 64
    out = []
    for pair in range(2):
        comps = halves(x[:, 128 * pair : 128 * pair + 128], parts)
        for upper in (False, True):
            if parts == 3:
                hi, mid, lo = comps
                if left:
                    a = side(low, hi, mid, upper).astype(BF)
                    pieces = [a, a, side(low, hi, lo, upper).astype(BF)]
                else:
                    pieces = [
                        side(low, hi, hi, upper).astype(BF),
                        side(low, mid, mid, upper).astype(BF),
                        side(low, lo, hi, upper).astype(BF),
                    ]
            else:
                hi, lo = comps
                if left:
                    a = side(low, hi, lo, upper).astype(BF)
                    pieces = [a, a]
                else:
                    pieces = [
                        side(low, hi, hi, upper).astype(BF),
                        side(low, lo, lo, upper).astype(BF),
                    ]
            out.append(jnp.concatenate(pieces, axis=1))
    return out


def dot_nt(a, b):
    return lax.dot_general(a, b, (((1,), (1,)), ((), ())), preferred_element_type=F32)


def dot_nn(a, b):
    return lax.dot_general(a, b, (((1,), (0,)), ((), ())), preferred_element_type=F32)


def two(x):
    hi = x.astype(BF)
    return hi, (x - hi.astype(F32)).astype(BF)


def heads_product(per_head, field):
    low = lax.broadcasted_iota(jnp.int32, (1, 128), 1) < 64
    rows, depth = per_head[0].shape
    hi, lo = two(field)
    if hi.shape[0] < depth:
        more = jnp.zeros((depth - hi.shape[0], 256), BF)
        hi, lo = jnp.concatenate([hi, more], axis=0), jnp.concatenate([lo, more], axis=0)
    out = []
    for pair in range(2):
        lanes = slice(128 * pair, 128 * pair + 128)
        left_hi, left_lo = two(jnp.concatenate(per_head[2 * pair : 2 * pair + 2], axis=0))
        both = jnp.concatenate([hi[:, lanes], lo[:, lanes]], axis=1)
        if depth == 128:
            below = jnp.concatenate([hi[:, lanes], jnp.zeros((depth, 128), BF)], axis=1)
            full = dot_nn(jnp.concatenate([left_hi, left_lo], axis=1), jnp.concatenate([both, below], axis=0))
            full = full[:, 0:128] + full[:, 128:256]
        else:
            full = dot_nn(left_hi, both)
            full = full[:, 0:128] + (full[:, 128:256] + dot_nn(left_lo, hi[:, lanes]))
        out.append(jnp.where(low, full[0:rows], full[rows : 2 * rows]))
    return jnp.concatenate(out, axis=1)


def attend(work, bias_ref, own_tokens, own_keys, inner):
    scores, dprobs = [], []
    for key_l, value_l, query_r, cot_r, _, _, _ in work:
        for head in range(HEADS):
            scores.append(dot_nt(key_l[head], query_r[head]) + bias_ref[...])
            dprobs.append(dot_nt(value_l[head], cot_r[head]))
    prob_rows, ds_rows, ds_cols = [], [], []
    for s, dp in zip(scores, dprobs):
        top = jnp.maximum(jnp.max(s, axis=0, keepdims=True), -1e29)
        e = jnp.exp(s - top)
        inv = 1.0 / jnp.maximum(jnp.sum(e, axis=0, keepdims=True), 1e-30)
        delta = inv * jnp.sum(e * dp, axis=0, keepdims=True)
        prob_rows.append(e[0:own_keys] * inv)
        ds = [e[part] * inv * (dp[part] - delta) for part in inner]
        ds_rows.append(ds[0][0:own_keys])
        ds = jnp.concatenate(ds, axis=0) if len(ds) > 1 else ds[0]
        ds_cols.append(ds[:, 0:own_tokens].T)
    out = []
    for image, (_, _, _, _, key, query, cot) in enumerate(work):
        here = slice(HEADS * image, HEADS * image + HEADS)
        out.append((
            heads_product(ds_cols[here], key) * 0.125,
            heads_product(ds_rows[here], query),
            heads_product(prob_rows[here], cot),
        ))
    return out


def rows(ref, first, count, pad=0):
    x = ref[first : first + count, :]
    return [x, jnp.zeros((pad, 256), F32)] if pad else [x]


CORNER = (0, 36, 72, 81)
REST = (0, 12, 24, 39)
SIDE = (0, 48, 96, 120)


def keep(ref, image, parts):
    count = parts[0].shape[0]
    for head in range(HEADS):
        first = (HEADS * image + head) * count
        ref[first : first + count, :] = parts[head]


def joined(image, refs, late, rows):
    out = []
    for head in range(HEADS):
        parts = []
        for ref, take in refs:
            count = ref.shape[0] // (2 * HEADS)
            first = (HEADS * image + head) * count
            parts.append(ref[first : first + take, :])
        parts.append(late[head])
        have = sum(x.shape[0] for x in parts)
        if have < rows:
            parts.append(jnp.zeros((rows - have, late[head].shape[1]), BF))
        out.append(jnp.concatenate(parts, axis=0))
    return out


def own_kernel(cols, own_q_ref, own_k_ref, own_v_ref, own_c_ref, even_bias_ref, odd_bias_ref, k_ref, v_ref, q_ref, c_ref):
    at = Places(cols)
    write_bias(
        even_bias_ref,
        ((at.own, 64, 64), (at.ha_in, 24, 24), (at.ha_out, 24, 24), (at.even_inner, 24, 24), (at.even_outer, 24, 24),
         (at.deven_in, 24, 24), (at.deven_out, 24, 24)),
        ((None, 0, 24), (lambda i: at.own(i, 3), 40, 40), (lambda i: at.ha_in(i, 3), 15, 16), (at.even_inner, 24, 24),
         (at.deven_in, 24, 24)),
    )
    write_bias(
        odd_bias_ref,
        ((at.own, 48, 48), (at.ha_in, 18, 24), (at.ha_out, 18, 24), (at.odd_inner, 24, 24), (at.odd_outer, 24, 24),
         (at.dodd_in, 9, 16), (at.dodd_out, 27, 32)),
        ((at.own, 24, 32), (at.ha_in, 9, 16), (at.odd_tokens, 24, 32), (at.dodd_in, 9, 16)),
    )
    for image in range(2):
        here = slice(64 * image, 64 * image + 64)
        keep(k_ref, image, stacked(own_k_ref[here, :], True, 3))
        keep(v_ref, image, stacked(own_v_ref[here, :], True, 2))
        keep(q_ref, image, stacked(own_q_ref[here, :] * 0.125, False, 3))
        keep(c_ref, image, stacked(own_c_ref[here, :], False, 2))


def ha_inner(image, corner_ref, rest_ref, field):
    return rows(corner_ref, 90 * image + CORNER[field], 18) + rows(rest_ref, 54 * image + REST[field], 6)


def ha_outer(image, corner_ref, rest_ref, field):
    return rows(corner_ref, 90 * image + CORNER[field] + 18, 18) + rows(rest_ref, 54 * image + REST[field] + 6, 6)


def odd_inner(image, odd_ref, odd_rest_ref, field):
    corner, rest = 90 * image + CORNER[field], 54 * image + REST[field]
    return rows(odd_ref, corner, 9) + rows(odd_ref, corner + 18, 9) + rows(odd_rest_ref, rest, 6)


def odd_outer(image, odd_ref, odd_rest_ref, field):
    corner, rest = 90 * image + CORNER[field], 54 * image + REST[field]
    return rows(odd_ref, corner + 9, 9) + rows(odd_ref, corner + 27, 9) + rows(odd_rest_ref, rest + 6, 6)


def odd_middle_tokens(image, corner_ref, odd_ref, odd_rest_ref, field):
    corner, rest = 90 * image + CORNER[field], 54 * image + REST[field]
    return rows(corner_ref, corner, 9, 7) + rows(odd_ref, corner, 9) + rows(odd_rest_ref, rest, 15, 8)


def middle_kernel(corner_ref, rest_ref, odd_ref, odd_rest_ref, even_k_ref, even_v_ref, even_q_ref, even_c_ref,
                  odd_k_ref, odd_v_ref, odd_q_ref, odd_c_ref):
    for image in range(2):
        for field, even_ref, odd_to_ref, parts in ((0, even_k_ref, odd_k_ref, 3), (1, even_v_ref, odd_v_ref, 2)):
            corner = 90 * image + CORNER[field]
            x = ha_inner(image, corner_ref, rest_ref, field) + ha_outer(image, corner_ref, rest_ref, field)
            keep(even_ref, image, stacked(jnp.concatenate(x, axis=0), True, parts))
            x = rows(corner_ref, corner, 18, 6) + rows(corner_ref, corner + 18, 18, 6)
            x += odd_inner(image, odd_ref, odd_rest_ref, field) + odd_outer(image, odd_ref, odd_rest_ref, field)
            keep(odd_to_ref, image, stacked(jnp.concatenate(x, axis=0), True, parts))
        for field, even_ref, odd_to_ref, parts, scale in (
            (2, even_q_ref, odd_q_ref, 3, 0.125), (3, even_c_ref, odd_c_ref, 2, 1.0),
        ):
            x = jnp.concatenate(rows(rest_ref, 54 * image + REST[field], 15, 1), axis=0)
            keep(even_ref, image, stacked(x * scale, False, parts))
            x = jnp.concatenate(odd_middle_tokens(image, corner_ref, odd_ref, odd_rest_ref, field), axis=0)
            keep(odd_to_ref, image, stacked(x * scale, False, parts))


def even_kernel(own_q_ref, own_k_ref, own_c_ref, corner_ref, rest_ref, even_ref, mate_ref, bias_ref,
                k0_ref, v0_ref, q0_ref, c0_ref, k1_ref, v1_ref, q1_ref, c1_ref, dq_ref, dk_ref, dv_ref):
    work = []
    for image in range(2):

        def mate_inner(field):
            return rows(mate_ref, 90 * image + CORNER[field], 18) + rows(mate_ref, 184 + 54 * image + REST[field], 6)

        def late_keys(field):
            even = 144 * image + SIDE[field]
            out = rows(even_ref, even, 48) + mate_inner(field)
            out += rows(mate_ref, 90 * image + CORNER[field] + 18, 18)
            out += rows(mate_ref, 184 + 54 * image + REST[field] + 6, 6)
            return jnp.concatenate(out, axis=0)

        def late_tokens(field):
            out = rows(even_ref, 144 * image + SIDE[field], 24)
            out += rows(mate_ref, 90 * image + CORNER[field], 9) + rows(mate_ref, 184 + 54 * image + REST[field], 15)
            return jnp.concatenate(out, axis=0)

        late_q, late_c = late_tokens(2) * 0.125, late_tokens(3)
        key = rows(own_k_ref, 64 * image, 64) + ha_inner(image, corner_ref, rest_ref, 0)
        key += rows(even_ref, 144 * image, 24) + mate_inner(0)
        query = rows(own_q_ref, 64 * image, 64) + rows(rest_ref, 54 * image + REST[2], 15, 1)
        cot = rows(own_c_ref, 64 * image, 64) + rows(rest_ref, 54 * image + REST[3], 15, 1)
        work.append((
            joined(image, ((k0_ref, 64), (k1_ref, 48)), stacked(late_keys(0), True, 3), 208),
            joined(image, ((v0_ref, 64), (v1_ref, 48)), stacked(late_keys(1), True, 2), 208),
            joined(image, ((q0_ref, 64), (q1_ref, 16)), stacked(late_q, False, 3), 128),
            joined(image, ((c0_ref, 64), (c1_ref, 16)), stacked(late_c, False, 2), 128),
            jnp.concatenate(key, axis=0),
            jnp.concatenate([jnp.concatenate(query, axis=0) * 0.125, late_q], axis=0),
            jnp.concatenate(cot + [late_c], axis=0),
        ))
    parts = attend(work, bias_ref, 64, 64, (slice(0, 88), slice(112, 136), slice(160, 184)))
    for image, (dq, dk, dv) in enumerate(parts):
        here = slice(64 * image, 64 * image + 64)
        dq_ref[here, :] = dq
        dk_ref[here, :] = dk
        dv_ref[here, :] = dv


def sort_kernel(cols, first_ref, second_ref, rest_ref, gate_ref, ha_ref, odd_ref, mate_ref):
    turned = by_row(lax.axis_index("wa"), cols)
    first, second = first_ref[...], second_ref[...]
    ha = jnp.where(turned, second, first)
    ha_ref[...] = ha
    odd_ref[...] = jnp.where(turned, first, second)
    mate_ref[0:184, :] = ha
    mate_ref[184:296, :] = rest_ref[...]


def release_kernel(message_ref, gate_ref, out_ref):
    out_ref[...] = message_ref[...]


def by_row(w, cols):
    return jnp.logical_and(((w + 1) >> 1) % 2 == 0, jnp.logical_and(w > 0, w < cols - 1))


def odd_kernel(own_q_ref, own_k_ref, own_c_ref, corner_ref, odd_ref, odd_rest_ref, far_ref, even_dq_ref, even_dk_ref,
               even_dv_ref, bias_ref, k0_ref, v0_ref, q0_ref, c0_ref, k1_ref, v1_ref, q1_ref, c1_ref,
               dq_ref, dk_ref, dv_ref, split_ref):
    p = lax.axis_index("wa") % 2
    work = []
    for image in range(2):

        def late_keys(field):
            corner = 90 * image + CORNER[field]
            return jnp.concatenate(rows(far_ref, corner, 9, 7) + rows(far_ref, corner + 9, 27, 5), axis=0)

        def late_tokens(field):
            return jnp.concatenate(rows(far_ref, 90 * image + CORNER[field], 9, 7), axis=0)

        late_q, late_c = late_tokens(2) * 0.125, late_tokens(3)
        late_k = late_keys(0)
        key = rows(own_k_ref, 64 * image, 48) + rows(corner_ref, 90 * image, 18, 6)
        key += odd_inner(image, odd_ref, odd_rest_ref, 0) + [late_k[0:16]]
        query = rows(own_q_ref, 64 * image, 32) + odd_middle_tokens(image, corner_ref, odd_ref, odd_rest_ref, 2)
        cot = rows(own_c_ref, 64 * image, 32) + odd_middle_tokens(image, corner_ref, odd_ref, odd_rest_ref, 3)
        work.append((
            joined(image, ((k0_ref, 48), (k1_ref, 96)), stacked(late_k, True, 3), 192),
            joined(image, ((v0_ref, 48), (v1_ref, 96)), stacked(late_keys(1), True, 2), 192),
            joined(image, ((q0_ref, 32), (q1_ref, 48)), stacked(late_q, False, 3), 128),
            joined(image, ((c0_ref, 32), (c1_ref, 48)), stacked(late_c, False, 2), 128),
            jnp.concatenate(key, axis=0),
            jnp.concatenate([jnp.concatenate(query, axis=0) * 0.125, late_q], axis=0),
            jnp.concatenate(cot + [late_c], axis=0),
        ))
    parts = attend(work, bias_ref, 24, 48, (slice(0, 72), slice(96, 120), slice(144, 160)))
    for image, (dq, dk, dv) in enumerate(parts):
        here = slice(64 * image, 64 * image + 64)
        none = jnp.zeros((16, 256), F32)
        results = (
            jnp.concatenate([dq, jnp.zeros((40, 256), F32)], axis=0) + even_dq_ref[here, :],
            jnp.concatenate([dk, none], axis=0) + even_dk_ref[here, :],
            jnp.concatenate([dv, none], axis=0) + even_dv_ref[here, :],
        )
        for index, x in enumerate(results):
            for slot in range(8):
                where = pl.ds(64 * image + slot_column(p, slot), 8, stride=8)
                for half in range(2):
                    split_ref[2 * index + half, where, :] = x[8 * slot : 8 * slot + 8, 128 * half : 128 * half + 128]
    for index, ref in enumerate((dq_ref, dk_ref, dv_ref)):
        for half in range(2):
            ref[:, 128 * half : 128 * half + 128] = split_ref[2 * index + half]


SMALL = pltpu.CompilerParams(vmem_limit_bytes=6 * 1024 * 1024)
OWN_US = 1
PREP_US = 1
FAR_US = 2
EVEN_US = 0


def cost(micros):
    return pl.CostEstimate(flops=int(micros * 1e9), bytes_accessed=int(micros * 3e6), transcendentals=0)


def per_device(queries, keys, values, cotangent):
    shape = queries.shape
    cols = lax.axis_size("wa")
    flat = [x.reshape(128, 256) for x in (queries, keys, values, cotangent)]
    to_corner, split = pl.pallas_call(
        corner_kernel, out_shape=(vmem(184), pltpu.VMEM((8, 128, 128), F32)), name="corner",
    )(flat[1], flat[2], flat[0], flat[3])
    to_rest, to_odd_rest, to_even, own_k, own_v, own_q, own_c = pl.pallas_call(
        pack_kernel, out_shape=(vmem(112), vmem(112), vmem(288)) + (vmem(128),) * 4, name="pack", compiler_params=SMALL,
    )(held(split))
    own = (own_q, own_k, own_v, own_c)

    both = ("ha", "wa")
    ends = (0, cols - 1)
    partner = {i: (i + 1 if i % 2 else i - 1) for i in range(cols) if i not in ends}
    first_pairs, second_pairs, far_pairs, odd_pairs = [], [], [], []
    for row in range(2):
        for col in range(cols):
            here, mate = row * cols + col, (1 - row) * cols + col
            beside = mate if col in ends else row * cols + partner[col]
            turned = (col + 1) // 2 % 2 == 0
            first_pairs.append((here, beside if turned else mate))
            far_pairs.append((here, mate if turned else beside))
            second_pairs.append((here, here if col in ends else mate if turned else beside))
            odd_pairs.append((here, beside))
    even_pairs = [(i, i ^ 1) for i in range(cols)]
    across = [(0, 1), (1, 0)]

    first = lax.ppermute(to_corner, both, first_pairs)
    second = lax.ppermute(to_corner, both, second_pairs)
    rest = lax.ppermute(to_rest, "ha", across)
    odd_rest = lax.ppermute(to_odd_rest, both, odd_pairs)
    to_even = pl.pallas_call(release_kernel, out_shape=vmem(288), name="release", compiler_params=SMALL)(held(to_even), held(first))
    even = lax.ppermute(to_even, "wa", even_pairs)
    far = lax.ppermute(first, both, far_pairs)
    each = 2 * HEADS

    def stacks(key_rows, token_rows):
        return (vmem(each * key_rows, 384, BF), vmem(each * key_rows, 256, BF), vmem(each * token_rows, 384, BF),
                vmem(each * token_rows, 256, BF))

    even_bias, odd_bias, *own_stacks = pl.pallas_call(
        functools.partial(own_kernel, cols),
        out_shape=(vmem(208, 128), vmem(192, 128)) + stacks(64, 64),
        compiler_params=SMALL,
        cost_estimate=cost(OWN_US),
        name="own",
    )(*[held(x) for x in own])
    corner, odd, to_mate = pl.pallas_call(
        functools.partial(sort_kernel, cols), out_shape=(vmem(184), vmem(184), vmem(296)), name="sort", compiler_params=SMALL,
    )(*[held(x) for x in (first, second, rest, even_bias)])
    mate = lax.ppermute(to_mate, "wa", even_pairs)
    middle = pl.pallas_call(
        middle_kernel,
        out_shape=stacks(48, 16) + stacks(96, 48),
        compiler_params=SMALL,
        cost_estimate=cost(PREP_US),
        name="middle",
    )(*[held(x) for x in (corner, rest, odd, odd_rest)])
    if FAR_US:
        far = pl.pallas_call(
            release_kernel, out_shape=vmem(184), cost_estimate=cost(FAR_US), name="arrive_far", compiler_params=SMALL,
        )(held(far), held(first))
    even_part = pl.pallas_call(
        even_kernel,
        out_shape=(vmem(128), vmem(128), vmem(128)),
        compiler_params=SMALL,
        cost_estimate=cost(EVEN_US),
        name="even_set",
    )(*[held(x) for x in (own_q, own_k, own_c, corner, rest, even, mate, even_bias, *own_stacks, *middle[0:4])])
    out = jax.ShapeDtypeStruct((128, 256), F32)
    grads = pl.pallas_call(
        odd_kernel,
        out_shape=(out, out, out),
        scratch_shapes=[pltpu.VMEM((6, 128, 128), F32)],
        compiler_params=SMALL,
        name="odd_set",
    )(*[held(x) for x in (own_q, own_k, own_c, corner, odd, odd_rest, far, *even_part, odd_bias, *own_stacks, *middle[4:8])])
    return tuple(g.reshape(shape) for g in grads)


def solution(mesh):
    spec = P(None, "ha", "wa", None)
    return jax.shard_map(
        per_device,
        mesh=mesh,
        in_specs=(spec,) * 4,
        out_specs=(spec,) * 3,
        check_vma=False,
    )
```

```python
import functools

import jax
import jax.numpy as jnp
from jax import lax
from jax.experimental import pallas as pl
from jax.experimental.pallas import tpu as pltpu
from jax.sharding import PartitionSpec as P

HEADS = 4
REACH = 3
FAR = 1000
NEG = -1e30
BF = jnp.bfloat16
F32 = jnp.float32


def vmem(rows, columns=256, dtype=F32):
    return pltpu.VMEM((rows, columns), dtype)


def held(x):
    return pltpu.with_memory_space_constraint(x, pltpu.VMEM)


def slot_column(p, slot):
    turned = jnp.where(slot < 3, slot + 5, jnp.where(slot < 6, slot - 1, slot - 6))
    return jnp.where(p == 0, slot, turned)


def pack_reader(split_ref):
    def col(index, image, column, first, count):
        rows = pl.ds(image * 64 + first * 8 + column, count, stride=8)
        return jnp.concatenate([split_ref[2 * index + half, rows, :] for half in range(2)], axis=1)

    return col


WIDE = (True, True, False, False)


def corner_kernel(k_ref, v_ref, q_ref, c_ref, corner_ref, split_ref):
    h = lax.axis_index("ha")
    p = lax.axis_index("wa") % 2
    row_in = jnp.where(h == 0, 5, 0)
    row_out = jnp.where(h == 0, 2, 3)
    col = pack_reader(split_ref)
    for index, ref in enumerate((k_ref, v_ref, q_ref, c_ref)):
        for half in range(2):
            split_ref[2 * index + half] = ref[:, 128 * half : 128 * half + 128]
    for image in range(2):
        at = 90 * image
        for index, wide in enumerate(WIDE):
            pieces = [(row_in, slot) for slot in range(6 if wide else 3)]
            pieces += [(row_out, slot) for slot in range(6)] if wide else []
            for first, slot in pieces:
                corner_ref[at : at + 3, :] = col(index, image, slot_column(p, slot), first, 3)
                at += 3


def pack_kernel(split_ref, rest_ref, odd_rest_ref, even_ref, own_k_ref, own_v_ref, own_q_ref, own_c_ref):
    h = lax.axis_index("ha")
    p = lax.axis_index("wa") % 2
    row_in = jnp.where(h == 0, 5, 0)
    row_out = jnp.where(h == 0, 2, 3)
    row_far = jnp.where(h == 0, 0, 6)
    row_rest = jnp.where(h == 0, 0, 3)
    even_in = jnp.where(p == 0, 5, 0)
    even_out = jnp.where(p == 0, 2, 3)
    slots = [slot_column(p, slot) for slot in range(8)]
    col = pack_reader(split_ref)
    for image in range(2):
        rest, odd_rest = 54 * image, 54 * image
        for index, wide in enumerate(WIDE):
            pieces = [(row_in, slot) for slot in ((6, 7) if wide else (3, 4, 5, 6, 7))]
            pieces += [(row_out, slot) for slot in (6, 7)] if wide else []
            for first, slot in pieces:
                rest_ref[rest : rest + 3, :] = col(index, image, slots[slot], first, 3)
                rest += 3
            for slot in range(6 if wide else 3):
                first, count = (row_far, 2) if wide else (row_rest, 5)
                odd_rest_ref[odd_rest : odd_rest + count, :] = col(index, image, slots[slot], first, count)
                odd_rest += count
    for image in range(2):
        at = 144 * image
        for index, (own_ref, wide) in enumerate(zip((own_k_ref, own_v_ref, own_q_ref, own_c_ref), WIDE)):
            for slot in range(8):
                own_ref[64 * image + 8 * slot : 64 * image + 8 * slot + 8, :] = col(index, image, slots[slot], 0, 8)
            for j in range(6 if wide else 3):
                even_ref[at + 8 * j : at + 8 * j + 8, :] = col(
                    index, image, even_in + j if j < 3 else even_out + j - 3, 0, 8
                )
            at += 48 if wide else 24


def third(i):
    return (i * 43) >> 7


class Places:
    def __init__(self, cols):
        h = lax.axis_index("ha")
        w = lax.axis_index("wa")
        self.p = p = w % 2
        lost = jnp.where(jnp.logical_or(w == 0, w == cols - 1), FAR, 0)
        self.row_in = jnp.where(h == 0, 8, -3)
        self.row_out = jnp.where(h == 0, 11, -6)
        self.even_in = jnp.where(p == 0, 8, -3)
        self.even_out = jnp.where(p == 0, 11, -6)
        self.even_all = jnp.where(p == 0, 8, -8)
        self.row_near = jnp.where(h == 0, 5, 0)
        self.row_next = jnp.where(h == 0, 2, 3)
        self.row_far = jnp.where(h == 0, 0, 6)
        self.row_rest = jnp.where(h == 0, 0, 3)
        self.odd_in = jnp.where(p == 0, -3, 8) + lost
        self.odd_out = jnp.where(p == 0, -6, 11) + lost

    def own(self, i, slot=0):
        return i & 7, slot_column(self.p, slot + (i >> 3))

    def ha_in(self, i, slot=0):
        j = third(i)
        return self.row_in + (i - 3 * j), slot_column(self.p, slot + j)

    def ha_out(self, i):
        j = third(i)
        return self.row_out + (i - 3 * j), slot_column(self.p, j)

    def deven_in(self, i):
        j = third(i)
        return self.row_in + (i - 3 * j), self.even_all + slot_column(1 - self.p, j)

    def deven_out(self, i):
        j = third(i)
        return self.row_out + (i - 3 * j), self.even_all + slot_column(1 - self.p, j)

    def even_inner(self, i):
        return i & 7, self.even_in + (i >> 3)

    def even_outer(self, i):
        return i & 7, self.even_out + (i >> 3)

    def odd_keys(self, i):
        k = jnp.where(i < 9, i, jnp.where(i < 18, i - 9, 0))
        j = third(k)
        row = jnp.where(i < 9, self.row_near, self.row_next) + (k - 3 * j)
        m = jnp.maximum(i - 18, 0)
        last = i >= 18
        return jnp.where(last, self.row_far + (m & 1), row), jnp.where(last, m >> 1, j)

    def odd_inner(self, i):
        row, j = self.odd_keys(i)
        return row, self.odd_in + j

    def odd_outer(self, i):
        row, j = self.odd_keys(i)
        return row, self.odd_out + j

    def odd_tokens(self, i):
        j = third(i)
        m = jnp.maximum(i - 9, 0)
        fifth = (m * 13) >> 6
        near = i < 9
        return (
            jnp.where(near, self.row_near + (i - 3 * j), self.row_rest + (m - 5 * fifth)),
            self.odd_in + jnp.where(near, j, fifth),
        )

    def dodd_in(self, i):
        j = third(i)
        return self.row_in + (i - 3 * j), self.odd_in + j

    def dodd_out(self, i):
        near = i < 9
        k = jnp.where(near, i, i - 9)
        j = third(k)
        row = jnp.where(near, self.row_in, self.row_out) + (k - 3 * j)
        column = jnp.where(
            near, self.odd_out + j, jnp.where(j < 3, self.odd_in + j, self.odd_out + j - 3)
        )
        return row, column


def write_bias(bias_ref, key_segments, token_segments):
    lane = lax.broadcasted_iota(jnp.int32, (8, 128), 1)
    token_r = jnp.full((8, 128), 3 * FAR, jnp.int32)
    token_c = jnp.full((8, 128), 3 * FAR, jnp.int32)
    first = 0
    for place, real, count in token_segments:
        if place is None:
            first += count
            continue
        r, c = place(jnp.clip(lane - first, 0, real - 1))
        inside = jnp.logical_and(lane >= first, lane < first + real)
        token_r = jnp.where(inside, r, token_r)
        token_c = jnp.where(inside, c, token_c)
        first += count
    width = bias_ref.shape[1]
    at = 0
    for place, real, count in key_segments:
        for group in range(count // 8):
            i = lax.broadcasted_iota(jnp.int32, (8, 128), 0) + 8 * group
            r, c = place(jnp.minimum(i, real - 1))
            if 8 * group + 8 > real:
                r = jnp.where(i < real, r, -FAR)
            near = jnp.logical_and(jnp.abs(r - token_r) <= REACH, jnp.abs(c - token_c) <= REACH)
            bias_ref[at : at + 8, :] = jnp.where(near, 0.0, NEG).astype(F32)[:, 0:width]
            at += 8


def rounded(x):
    return x.astype(BF).astype(F32)


def halves(x, parts):
    out = []
    for part in range(parts):
        top = rounded(x)
        out.append((top, pltpu.roll(top, 64, 1)))
        if part + 1 < parts:
            x = x - top
    return out


def side(low, a, b, upper):
    if upper:
        return jnp.where(low, b[1], a[0])
    return jnp.where(low, a[0], b[1])


def stacked(x, left, parts):
    low = lax.broadcasted_iota(jnp.int32, (1, 128), 1) < 64
    out = []
    for pair in range(2):
        comps = halves(x[:, 128 * pair : 128 * pair + 128], parts)
        for upper in (False, True):
            if parts == 3:
                hi, mid, lo = comps
                if left:
                    a = side(low, hi, mid, upper).astype(BF)
                    pieces = [a, a, side(low, hi, lo, upper).astype(BF)]
                else:
                    pieces = [
                        side(low, hi, hi, upper).astype(BF),
                        side(low, mid, mid, upper).astype(BF),
                        side(low, lo, hi, upper).astype(BF),
                    ]
            else:
                hi, lo = comps
                if left:
                    a = side(low, hi, lo, upper).astype(BF)
                    pieces = [a, a]
                else:
                    pieces = [
                        side(low, hi, hi, upper).astype(BF),
                        side(low, lo, lo, upper).astype(BF),
                    ]
            out.append(jnp.concatenate(pieces, axis=1))
    return out


def dot_nt(a, b):
    return lax.dot_general(a, b, (((1,), (1,)), ((), ())), preferred_element_type=F32)


def dot_nn(a, b):
    return lax.dot_general(a, b, (((1,), (0,)), ((), ())), preferred_element_type=F32)


def two(x):
    hi = x.astype(BF)
    return hi, (x - hi.astype(F32)).astype(BF)


def heads_product(per_head, field):
    low = lax.broadcasted_iota(jnp.int32, (1, 128), 1) < 64
    rows, depth = per_head[0].shape
    hi, lo = two(field)
    if hi.shape[0] < depth:
        more = jnp.zeros((depth - hi.shape[0], 256), BF)
        hi, lo = jnp.concatenate([hi, more], axis=0), jnp.concatenate([lo, more], axis=0)
    out = []
    for pair in range(2):
        lanes = slice(128 * pair, 128 * pair + 128)
        left_hi, left_lo = two(jnp.concatenate(per_head[2 * pair : 2 * pair + 2], axis=0))
        both = jnp.concatenate([hi[:, lanes], lo[:, lanes]], axis=1)
        if depth == 128:
            below = jnp.concatenate([hi[:, lanes], jnp.zeros((depth, 128), BF)], axis=1)
            full = dot_nn(jnp.concatenate([left_hi, left_lo], axis=1), jnp.concatenate([both, below], axis=0))
            full = full[:, 0:128] + full[:, 128:256]
        else:
            full = dot_nn(left_hi, both)
            full = full[:, 0:128] + (full[:, 128:256] + dot_nn(left_lo, hi[:, lanes]))
        out.append(jnp.where(low, full[0:rows], full[rows : 2 * rows]))
    return jnp.concatenate(out, axis=1)


def attend(work):
    scores, dprobs = [], []
    for key_l, value_l, query_r, cot_r, *_, bias_ref, _, _, _ in work:
        for head in range(HEADS):
            scores.append(dot_nt(key_l[head], query_r[head]) + bias_ref[...])
            dprobs.append(dot_nt(value_l[head], cot_r[head]))
    prob_rows, ds_rows, ds_cols = [], [], []
    for item, (*_, own_tokens, own_keys, inner) in enumerate(work):
        for head in range(HEADS):
            s, dp = scores[HEADS * item + head], dprobs[HEADS * item + head]
            top = jnp.maximum(jnp.max(s, axis=0, keepdims=True), -1e29)
            e = jnp.exp(s - top)
            inv = 1.0 / jnp.maximum(jnp.sum(e, axis=0, keepdims=True), 1e-30)
            delta = inv * jnp.sum(e * dp, axis=0, keepdims=True)
            prob_rows.append(e[0:own_keys] * inv)
            ds = [e[part] * inv * (dp[part] - delta) for part in inner]
            ds_rows.append(ds[0][0:own_keys])
            ds = jnp.concatenate(ds, axis=0) if len(ds) > 1 else ds[0]
            ds_cols.append(ds[:, 0:own_tokens].T)
    out = []
    for item, (_, _, _, _, key, query, cot, *_) in enumerate(work):
        here = slice(HEADS * item, HEADS * item + HEADS)
        out.append((
            heads_product(ds_cols[here], key) * 0.125,
            heads_product(ds_rows[here], query),
            heads_product(prob_rows[here], cot),
        ))
    return out


def rows(ref, first, count, pad=0):
    x = ref[first : first + count, :]
    return [x, jnp.zeros((pad, 256), F32)] if pad else [x]


CORNER = (0, 36, 72, 81)
REST = (0, 12, 24, 39)
SIDE = (0, 48, 96, 120)


def keep(ref, image, parts):
    count = parts[0].shape[0]
    for head in range(HEADS):
        first = (HEADS * image + head) * count
        ref[first : first + count, :] = parts[head]


def joined(image, refs, late, rows):
    out = []
    for head in range(HEADS):
        parts = []
        for ref, take in refs:
            count = ref.shape[0] // (2 * HEADS)
            first = (HEADS * image + head) * count
            parts.append(ref[first : first + take, :])
        parts.append(late[head])
        have = sum(x.shape[0] for x in parts)
        if have < rows:
            parts.append(jnp.zeros((rows - have, late[head].shape[1]), BF))
        out.append(jnp.concatenate(parts, axis=0))
    return out


def own_kernel(cols, own_q_ref, own_k_ref, own_v_ref, own_c_ref, even_bias_ref, odd_bias_ref, k_ref, v_ref, q_ref, c_ref):
    at = Places(cols)
    write_bias(
        even_bias_ref,
        ((at.own, 64, 64), (at.ha_in, 24, 24), (at.ha_out, 24, 24), (at.even_inner, 24, 24), (at.even_outer, 24, 24),
         (at.deven_in, 24, 24), (at.deven_out, 24, 24)),
        ((None, 0, 24), (lambda i: at.own(i, 3), 40, 40), (lambda i: at.ha_in(i, 3), 15, 16), (at.even_inner, 24, 24),
         (at.deven_in, 24, 24)),
    )
    write_bias(
        odd_bias_ref,
        ((at.own, 48, 48), (at.ha_in, 18, 24), (at.ha_out, 18, 24), (at.odd_inner, 24, 24), (at.odd_outer, 24, 24),
         (at.dodd_in, 9, 16), (at.dodd_out, 27, 32)),
        ((at.own, 24, 32), (at.ha_in, 9, 16), (at.odd_tokens, 24, 32), (at.dodd_in, 9, 16)),
    )
    for image in range(2):
        here = slice(64 * image, 64 * image + 64)
        keep(k_ref, image, stacked(own_k_ref[here, :], True, 3))
        keep(v_ref, image, stacked(own_v_ref[here, :], True, 2))
        keep(q_ref, image, stacked(own_q_ref[here, :] * 0.125, False, 3))
        keep(c_ref, image, stacked(own_c_ref[here, :], False, 2))


def ha_inner(image, corner_ref, rest_ref, field):
    return rows(corner_ref, 90 * image + CORNER[field], 18) + rows(rest_ref, 54 * image + REST[field], 6)


def ha_outer(image, corner_ref, rest_ref, field):
    return rows(corner_ref, 90 * image + CORNER[field] + 18, 18) + rows(rest_ref, 54 * image + REST[field] + 6, 6)


def odd_inner(image, odd_ref, odd_rest_ref, field):
    corner, rest = 90 * image + CORNER[field], 54 * image + REST[field]
    return rows(odd_ref, corner, 9) + rows(odd_ref, corner + 18, 9) + rows(odd_rest_ref, rest, 6)


def odd_outer(image, odd_ref, odd_rest_ref, field):
    corner, rest = 90 * image + CORNER[field], 54 * image + REST[field]
    return rows(odd_ref, corner + 9, 9) + rows(odd_ref, corner + 27, 9) + rows(odd_rest_ref, rest + 6, 6)


def odd_middle_tokens(image, corner_ref, odd_ref, odd_rest_ref, field):
    corner, rest = 90 * image + CORNER[field], 54 * image + REST[field]
    return rows(corner_ref, corner, 9, 7) + rows(odd_ref, corner, 9) + rows(odd_rest_ref, rest, 15, 8)


def middle_kernel(corner_ref, rest_ref, odd_ref, odd_rest_ref, even_k_ref, even_v_ref, even_q_ref, even_c_ref,
                  odd_k_ref, odd_v_ref, odd_q_ref, odd_c_ref):
    for image in range(2):
        for field, even_ref, odd_to_ref, parts in ((0, even_k_ref, odd_k_ref, 3), (1, even_v_ref, odd_v_ref, 2)):
            corner = 90 * image + CORNER[field]
            x = ha_inner(image, corner_ref, rest_ref, field) + ha_outer(image, corner_ref, rest_ref, field)
            keep(even_ref, image, stacked(jnp.concatenate(x, axis=0), True, parts))
            x = rows(corner_ref, corner, 18, 6) + rows(corner_ref, corner + 18, 18, 6)
            x += odd_inner(image, odd_ref, odd_rest_ref, field) + odd_outer(image, odd_ref, odd_rest_ref, field)
            keep(odd_to_ref, image, stacked(jnp.concatenate(x, axis=0), True, parts))
        for field, even_ref, odd_to_ref, parts, scale in (
            (2, even_q_ref, odd_q_ref, 3, 0.125), (3, even_c_ref, odd_c_ref, 2, 1.0),
        ):
            x = jnp.concatenate(rows(rest_ref, 54 * image + REST[field], 15, 1), axis=0)
            keep(even_ref, image, stacked(x * scale, False, parts))
            x = jnp.concatenate(odd_middle_tokens(image, corner_ref, odd_ref, odd_rest_ref, field), axis=0)
            keep(odd_to_ref, image, stacked(x * scale, False, parts))


def even_work(own_q_ref, own_k_ref, own_c_ref, corner_ref, rest_ref, even_ref, mate_ref, bias_ref,
                k0_ref, v0_ref, q0_ref, c0_ref, k1_ref, v1_ref, q1_ref, c1_ref):
    work = []
    for image in range(2):

        def mate_inner(field):
            return rows(mate_ref, 90 * image + CORNER[field], 18) + rows(mate_ref, 184 + 54 * image + REST[field], 6)

        def late_keys(field):
            even = 144 * image + SIDE[field]
            out = rows(even_ref, even, 48) + mate_inner(field)
            out += rows(mate_ref, 90 * image + CORNER[field] + 18, 18)
            out += rows(mate_ref, 184 + 54 * image + REST[field] + 6, 6)
            return jnp.concatenate(out, axis=0)

        def late_tokens(field):
            out = rows(even_ref, 144 * image + SIDE[field], 24)
            out += rows(mate_ref, 90 * image + CORNER[field], 9) + rows(mate_ref, 184 + 54 * image + REST[field], 15)
            return jnp.concatenate(out, axis=0)

        late_q, late_c = late_tokens(2) * 0.125, late_tokens(3)
        key = rows(own_k_ref, 64 * image, 64) + ha_inner(image, corner_ref, rest_ref, 0)
        key += rows(even_ref, 144 * image, 24) + mate_inner(0)
        query = rows(own_q_ref, 64 * image, 64) + rows(rest_ref, 54 * image + REST[2], 15, 1)
        cot = rows(own_c_ref, 64 * image, 64) + rows(rest_ref, 54 * image + REST[3], 15, 1)
        work.append((
            joined(image, ((k0_ref, 64), (k1_ref, 48)), stacked(late_keys(0), True, 3), 208),
            joined(image, ((v0_ref, 64), (v1_ref, 48)), stacked(late_keys(1), True, 2), 208),
            joined(image, ((q0_ref, 64), (q1_ref, 16)), stacked(late_q, False, 3), 128),
            joined(image, ((c0_ref, 64), (c1_ref, 16)), stacked(late_c, False, 2), 128),
            jnp.concatenate(key, axis=0),
            jnp.concatenate([jnp.concatenate(query, axis=0) * 0.125, late_q], axis=0),
            jnp.concatenate(cot + [late_c], axis=0),
            bias_ref, 64, 64, (slice(0, 88), slice(112, 136), slice(160, 184)),
        ))
    return work


def sort_kernel(cols, first_ref, second_ref, rest_ref, gate_ref, ha_ref, odd_ref, mate_ref):
    turned = by_row(lax.axis_index("wa"), cols)
    first, second = first_ref[...], second_ref[...]
    ha = jnp.where(turned, second, first)
    ha_ref[...] = ha
    odd_ref[...] = jnp.where(turned, first, second)
    mate_ref[0:184, :] = ha
    mate_ref[184:296, :] = rest_ref[...]


def release_kernel(message_ref, gate_ref, out_ref):
    out_ref[...] = message_ref[...]


def by_row(w, cols):
    return jnp.logical_and(((w + 1) >> 1) % 2 == 0, jnp.logical_and(w > 0, w < cols - 1))


def odd_work(own_q_ref, own_k_ref, own_c_ref, corner_ref, odd_ref, odd_rest_ref, far_ref, bias_ref, k0_ref, v0_ref, q0_ref, c0_ref, k1_ref, v1_ref, q1_ref, c1_ref):
    work = []
    for image in range(2):

        def late_keys(field):
            corner = 90 * image + CORNER[field]
            return jnp.concatenate(rows(far_ref, corner, 9, 7) + rows(far_ref, corner + 9, 27, 5), axis=0)

        def late_tokens(field):
            return jnp.concatenate(rows(far_ref, 90 * image + CORNER[field], 9, 7), axis=0)

        late_q, late_c = late_tokens(2) * 0.125, late_tokens(3)
        late_k = late_keys(0)
        key = rows(own_k_ref, 64 * image, 48) + rows(corner_ref, 90 * image, 18, 6)
        key += odd_inner(image, odd_ref, odd_rest_ref, 0) + [late_k[0:16]]
        query = rows(own_q_ref, 64 * image, 32) + odd_middle_tokens(image, corner_ref, odd_ref, odd_rest_ref, 2)
        cot = rows(own_c_ref, 64 * image, 32) + odd_middle_tokens(image, corner_ref, odd_ref, odd_rest_ref, 3)
        work.append((
            joined(image, ((k0_ref, 48), (k1_ref, 96)), stacked(late_k, True, 3), 192),
            joined(image, ((v0_ref, 48), (v1_ref, 96)), stacked(late_keys(1), True, 2), 192),
            joined(image, ((q0_ref, 32), (q1_ref, 48)), stacked(late_q, False, 3), 128),
            joined(image, ((c0_ref, 32), (c1_ref, 48)), stacked(late_c, False, 2), 128),
            jnp.concatenate(key, axis=0),
            jnp.concatenate([jnp.concatenate(query, axis=0) * 0.125, late_q], axis=0),
            jnp.concatenate(cot + [late_c], axis=0),
            bias_ref, 24, 48, (slice(0, 72), slice(96, 120), slice(144, 160)),
        ))
    return work


def last_kernel(own_q_ref, own_k_ref, own_c_ref, corner_ref, rest_ref, even_ref, mate_ref, odd_ref, odd_rest_ref, far_ref,
                even_bias_ref, odd_bias_ref, k0_ref, v0_ref, q0_ref, c0_ref, k1_ref, v1_ref, q1_ref, c1_ref,
                k2_ref, v2_ref, q2_ref, c2_ref, dq_ref, dk_ref, dv_ref, split_ref):
    p = lax.axis_index("wa") % 2
    own = (own_q_ref, own_k_ref, own_c_ref)
    kept = (k0_ref, v0_ref, q0_ref, c0_ref)
    work = even_work(*own, corner_ref, rest_ref, even_ref, mate_ref, even_bias_ref, *kept, k1_ref, v1_ref, q1_ref, c1_ref)
    work += odd_work(*own, corner_ref, odd_ref, odd_rest_ref, far_ref, odd_bias_ref, *kept, k2_ref, v2_ref, q2_ref, c2_ref)
    parts = attend(work)
    for image in range(2):
        even_dq, even_dk, even_dv = parts[image]
        dq, dk, dv = parts[2 + image]
        none = jnp.zeros((16, 256), F32)
        results = (
            jnp.concatenate([dq, jnp.zeros((40, 256), F32)], axis=0) + even_dq,
            jnp.concatenate([dk, none], axis=0) + even_dk,
            jnp.concatenate([dv, none], axis=0) + even_dv,
        )
        for index, x in enumerate(results):
            for slot in range(8):
                where = pl.ds(64 * image + slot_column(p, slot), 8, stride=8)
                for half in range(2):
                    split_ref[2 * index + half, where, :] = x[8 * slot : 8 * slot + 8, 128 * half : 128 * half + 128]
    for index, ref in enumerate((dq_ref, dk_ref, dv_ref)):
        for half in range(2):
            ref[:, 128 * half : 128 * half + 128] = split_ref[2 * index + half]


SMALL = pltpu.CompilerParams(vmem_limit_bytes=6 * 1024 * 1024)
LARGE = pltpu.CompilerParams(vmem_limit_bytes=12 * 1024 * 1024)
OWN_US = 0
PREP_US = 1
FAR_US = 2


def cost(micros):
    return pl.CostEstimate(flops=int(micros * 1e9), bytes_accessed=int(micros * 3e6), transcendentals=0)


def per_device(queries, keys, values, cotangent):
    shape = queries.shape
    cols = lax.axis_size("wa")
    flat = [x.reshape(128, 256) for x in (queries, keys, values, cotangent)]
    to_corner, split = pl.pallas_call(
        corner_kernel, out_shape=(vmem(184), pltpu.VMEM((8, 128, 128), F32)), name="corner",
    )(flat[1], flat[2], flat[0], flat[3])
    to_rest, to_odd_rest, to_even, own_k, own_v, own_q, own_c = pl.pallas_call(
        pack_kernel, out_shape=(vmem(112), vmem(112), vmem(288)) + (vmem(128),) * 4, name="pack", compiler_params=SMALL,
    )(held(split))
    own = (own_q, own_k, own_v, own_c)

    both = ("ha", "wa")
    ends = (0, cols - 1)
    partner = {i: (i + 1 if i % 2 else i - 1) for i in range(cols) if i not in ends}
    first_pairs, second_pairs, far_pairs, odd_pairs = [], [], [], []
    for row in range(2):
        for col in range(cols):
            here, mate = row * cols + col, (1 - row) * cols + col
            beside = mate if col in ends else row * cols + partner[col]
            turned = (col + 1) // 2 % 2 == 0
            first_pairs.append((here, beside if turned else mate))
            far_pairs.append((here, mate if turned else beside))
            second_pairs.append((here, here if col in ends else mate if turned else beside))
            odd_pairs.append((here, beside))
    even_pairs = [(i, i ^ 1) for i in range(cols)]
    across = [(0, 1), (1, 0)]

    first = lax.ppermute(to_corner, both, first_pairs)
    second = lax.ppermute(to_corner, both, second_pairs)
    rest = lax.ppermute(to_rest, "ha", across)
    odd_rest = lax.ppermute(to_odd_rest, both, odd_pairs)
    to_even = pl.pallas_call(release_kernel, out_shape=vmem(288), name="release", compiler_params=SMALL)(held(to_even), held(first))
    even = lax.ppermute(to_even, "wa", even_pairs)
    far = lax.ppermute(first, both, far_pairs)
    each = 2 * HEADS

    def stacks(key_rows, token_rows):
        return (vmem(each * key_rows, 384, BF), vmem(each * key_rows, 256, BF), vmem(each * token_rows, 384, BF),
                vmem(each * token_rows, 256, BF))

    even_bias, odd_bias, *own_stacks = pl.pallas_call(
        functools.partial(own_kernel, cols),
        out_shape=(vmem(208, 128), vmem(192, 128)) + stacks(64, 64),
        compiler_params=SMALL,
        cost_estimate=cost(OWN_US),
        name="own",
    )(*[held(x) for x in own])
    corner, odd, to_mate = pl.pallas_call(
        functools.partial(sort_kernel, cols), out_shape=(vmem(184), vmem(184), vmem(296)), name="sort", compiler_params=SMALL,
    )(*[held(x) for x in (first, second, rest, even_bias)])
    mate = lax.ppermute(to_mate, "wa", even_pairs)
    middle = pl.pallas_call(
        middle_kernel,
        out_shape=stacks(48, 16) + stacks(96, 48),
        compiler_params=SMALL,
        cost_estimate=cost(PREP_US),
        name="middle",
    )(*[held(x) for x in (corner, rest, odd, odd_rest)])
    if FAR_US:
        far = pl.pallas_call(
            release_kernel, out_shape=vmem(184), cost_estimate=cost(FAR_US), name="arrive_far", compiler_params=SMALL,
        )(held(far), held(first))
    out = jax.ShapeDtypeStruct((128, 256), F32)
    grads = pl.pallas_call(
        last_kernel,
        out_shape=(out, out, out),
        scratch_shapes=[pltpu.VMEM((6, 128, 128), F32)],
        compiler_params=LARGE,
        name="attend",
    )(*[held(x) for x in (own_q, own_k, own_c, corner, rest, even, mate, odd, odd_rest, far, even_bias, odd_bias,
                          *own_stacks, *middle)])
    return tuple(g.reshape(shape) for g in grads)


def solution(mesh):
    spec = P(None, "ha", "wa", None)
    return jax.shard_map(
        per_device,
        mesh=mesh,
        in_specs=(spec,) * 4,
        out_specs=(spec,) * 3,
        check_vma=False,
    )
```

```python
import functools

import jax
import jax.numpy as jnp
from jax import lax
from jax.experimental import pallas as pl
from jax.experimental.pallas import tpu as pltpu
from jax.sharding import PartitionSpec as P

HEADS = 4
REACH = 3
FAR = 1000
NEG = -1e30
BF = jnp.bfloat16
F32 = jnp.float32


def vmem(rows, columns=256, dtype=F32):
    return pltpu.VMEM((rows, columns), dtype)


def held(x):
    return pltpu.with_memory_space_constraint(x, pltpu.VMEM)


def slot_column(p, slot):
    turned = jnp.where(slot < 3, slot + 5, jnp.where(slot < 6, slot - 1, slot - 6))
    return jnp.where(p == 0, slot, turned)


def pack_reader(split_ref):
    def col(index, image, column, first, count):
        rows = pl.ds(image * 64 + first * 8 + column, count, stride=8)
        return jnp.concatenate([split_ref[2 * index + half, rows, :] for half in range(2)], axis=1)

    return col


WIDE = (True, True, False, False)

SPLIT = 136


def corner_kernel(k_ref, v_ref, q_ref, c_ref, corner_ref, split_ref):
    h = lax.axis_index("ha")
    p = lax.axis_index("wa") % 2
    row_in = jnp.where(h == 0, 5, 0)
    row_out = jnp.where(h == 0, 2, 3)
    col = pack_reader(split_ref)
    for index, ref in enumerate((k_ref, v_ref, q_ref, c_ref)):
        for half in range(2):
            split_ref[2 * index + half, 0:128, :] = ref[:, 128 * half : 128 * half + 128]
    for image in range(2):
        at = 90 * image
        for index, wide in enumerate(WIDE):
            pieces = [(row_in, slot) for slot in range(6 if wide else 3)]
            pieces += [(row_out, slot) for slot in range(6)] if wide else []
            for first, slot in pieces:
                corner_ref[at : at + 3, :] = col(index, image, slot_column(p, slot), first, 3)
                at += 3


def pack_kernel(split_ref, rest_ref, odd_rest_ref, even_ref, own_k_ref, own_v_ref, own_q_ref, own_c_ref):
    h = lax.axis_index("ha")
    p = lax.axis_index("wa") % 2
    row_in = jnp.where(h == 0, 5, 0)
    row_out = jnp.where(h == 0, 2, 3)
    row_far = jnp.where(h == 0, 0, 6)
    row_rest = jnp.where(h == 0, 0, 3)
    even_in = jnp.where(p == 0, 5, 0)
    even_out = jnp.where(p == 0, 2, 3)
    slots = [slot_column(p, slot) for slot in range(8)]
    col = pack_reader(split_ref)
    for image in range(2):
        rest, odd_rest = 54 * image, 54 * image
        for index, wide in enumerate(WIDE):
            pieces = [(row_in, slot) for slot in ((6, 7) if wide else (3, 4, 5, 6, 7))]
            pieces += [(row_out, slot) for slot in (6, 7)] if wide else []
            for first, slot in pieces:
                rest_ref[rest : rest + 3, :] = col(index, image, slots[slot], first, 3)
                rest += 3
            for slot in range(6 if wide else 3):
                first, count = (row_far, 2) if wide else (row_rest, 5)
                odd_rest_ref[odd_rest : odd_rest + count, :] = col(index, image, slots[slot], first, count)
                odd_rest += count
    for image in range(2):
        at = 144 * image
        for index, (own_ref, wide) in enumerate(zip((own_k_ref, own_v_ref, own_q_ref, own_c_ref), WIDE)):
            for slot in range(8):
                own_ref[64 * image + 8 * slot : 64 * image + 8 * slot + 8, :] = col(index, image, slots[slot], 0, 8)
            for j in range(6 if wide else 3):
                even_ref[at + 8 * j : at + 8 * j + 8, :] = col(
                    index, image, even_in + j if j < 3 else even_out + j - 3, 0, 8
                )
            at += 48 if wide else 24


def third(i):
    return (i * 43) >> 7


class Places:
    def __init__(self, cols):
        h = lax.axis_index("ha")
        w = lax.axis_index("wa")
        self.p = p = w % 2
        lost = jnp.where(jnp.logical_or(w == 0, w == cols - 1), FAR, 0)
        self.row_in = jnp.where(h == 0, 8, -3)
        self.row_out = jnp.where(h == 0, 11, -6)
        self.even_in = jnp.where(p == 0, 8, -3)
        self.even_out = jnp.where(p == 0, 11, -6)
        self.even_all = jnp.where(p == 0, 8, -8)
        self.row_near = jnp.where(h == 0, 5, 0)
        self.row_next = jnp.where(h == 0, 2, 3)
        self.row_far = jnp.where(h == 0, 0, 6)
        self.row_rest = jnp.where(h == 0, 0, 3)
        self.odd_in = jnp.where(p == 0, -3, 8) + lost
        self.odd_out = jnp.where(p == 0, -6, 11) + lost

    def own(self, i, slot=0):
        return i & 7, slot_column(self.p, slot + (i >> 3))

    def ha_in(self, i, slot=0):
        j = third(i)
        return self.row_in + (i - 3 * j), slot_column(self.p, slot + j)

    def ha_out(self, i):
        j = third(i)
        return self.row_out + (i - 3 * j), slot_column(self.p, j)

    def mate_in(self, i):
        j = third(i)
        slot = jnp.where(j < 5, j + 3, j - 5)
        return self.row_in + (i - 3 * j), self.even_all + slot_column(1 - self.p, slot)

    def deven_in(self, i):
        j = third(i)
        return self.row_in + (i - 3 * j), self.even_all + slot_column(1 - self.p, j)

    def deven_out(self, i):
        j = third(i)
        return self.row_out + (i - 3 * j), self.even_all + slot_column(1 - self.p, j)

    def even_inner(self, i):
        return i & 7, self.even_in + (i >> 3)

    def even_outer(self, i):
        return i & 7, self.even_out + (i >> 3)

    def odd_keys(self, i):
        k = jnp.where(i < 9, i, jnp.where(i < 18, i - 9, 0))
        j = third(k)
        row = jnp.where(i < 9, self.row_near, self.row_next) + (k - 3 * j)
        m = jnp.maximum(i - 18, 0)
        last = i >= 18
        return jnp.where(last, self.row_far + (m & 1), row), jnp.where(last, m >> 1, j)

    def odd_inner(self, i):
        row, j = self.odd_keys(i)
        return row, self.odd_in + j

    def odd_outer(self, i):
        row, j = self.odd_keys(i)
        return row, self.odd_out + j

    def odd_tokens(self, i):
        j = third(i)
        m = jnp.maximum(i - 9, 0)
        fifth = (m * 13) >> 6
        near = i < 9
        return (
            jnp.where(near, self.row_near + (i - 3 * j), self.row_rest + (m - 5 * fifth)),
            self.odd_in + jnp.where(near, j, fifth),
        )

    def dodd_in(self, i):
        j = third(i)
        return self.row_in + (i - 3 * j), self.odd_in + j

    def dodd_out(self, i):
        near = i < 9
        k = jnp.where(near, i, i - 9)
        j = third(k)
        row = jnp.where(near, self.row_in, self.row_out) + (k - 3 * j)
        column = jnp.where(
            near, self.odd_out + j, jnp.where(j < 3, self.odd_in + j, self.odd_out + j - 3)
        )
        return row, column


def write_bias(bias_ref, key_segments, token_segments):
    lane = lax.broadcasted_iota(jnp.int32, (8, 128), 1)
    token_r = jnp.full((8, 128), 3 * FAR, jnp.int32)
    token_c = jnp.full((8, 128), 3 * FAR, jnp.int32)
    first = 0
    for place, real, count in token_segments:
        if place is None:
            first += count
            continue
        r, c = place(jnp.clip(lane - first, 0, real - 1))
        inside = jnp.logical_and(lane >= first, lane < first + real)
        token_r = jnp.where(inside, r, token_r)
        token_c = jnp.where(inside, c, token_c)
        first += count
    width = bias_ref.shape[1]
    at = 0
    for place, real, count in key_segments:
        for group in range(count // 8):
            i = lax.broadcasted_iota(jnp.int32, (8, 128), 0) + 8 * group
            r, c = place(jnp.minimum(i, real - 1))
            if 8 * group + 8 > real:
                r = jnp.where(i < real, r, -FAR)
            near = jnp.logical_and(jnp.abs(r - token_r) <= REACH, jnp.abs(c - token_c) <= REACH)
            bias_ref[at : at + 8, :] = jnp.where(near, 0.0, NEG).astype(F32)[:, 0:width]
            at += 8


def rounded(x):
    return x.astype(BF).astype(F32)


def halves(x, parts):
    out = []
    for part in range(parts):
        top = rounded(x)
        out.append((top, pltpu.roll(top, 64, 1)))
        if part + 1 < parts:
            x = x - top
    return out


def side(low, a, b, upper):
    if upper:
        return jnp.where(low, b[1], a[0])
    return jnp.where(low, a[0], b[1])


def stacked(x, left, parts):
    low = lax.broadcasted_iota(jnp.int32, (1, 128), 1) < 64
    out = []
    for pair in range(2):
        comps = halves(x[:, 128 * pair : 128 * pair + 128], parts)
        for upper in (False, True):
            if parts == 3:
                hi, mid, lo = comps
                if left:
                    a = side(low, hi, mid, upper).astype(BF)
                    pieces = [a, a, side(low, hi, lo, upper).astype(BF)]
                else:
                    pieces = [
                        side(low, hi, hi, upper).astype(BF),
                        side(low, mid, mid, upper).astype(BF),
                        side(low, lo, hi, upper).astype(BF),
                    ]
            else:
                hi, lo = comps
                if left:
                    a = side(low, hi, lo, upper).astype(BF)
                    pieces = [a, a]
                else:
                    pieces = [
                        side(low, hi, hi, upper).astype(BF),
                        side(low, lo, lo, upper).astype(BF),
                    ]
            out.append(jnp.concatenate(pieces, axis=1))
    return out


def dot_nt(a, b):
    return lax.dot_general(a, b, (((1,), (1,)), ((), ())), preferred_element_type=F32)


def dot_nn(a, b):
    return lax.dot_general(a, b, (((1,), (0,)), ((), ())), preferred_element_type=F32)


def two(x):
    hi = x.astype(BF)
    return hi, (x - hi.astype(F32)).astype(BF)


def heads_product(per_head, field):
    low = lax.broadcasted_iota(jnp.int32, (1, 128), 1) < 64
    rows, depth = per_head[0].shape
    hi, lo = two(field)
    if hi.shape[0] < depth:
        more = jnp.zeros((depth - hi.shape[0], 256), BF)
        hi, lo = jnp.concatenate([hi, more], axis=0), jnp.concatenate([lo, more], axis=0)
    out = []
    for pair in range(2):
        lanes = slice(128 * pair, 128 * pair + 128)
        left_hi, left_lo = two(jnp.concatenate(per_head[2 * pair : 2 * pair + 2], axis=0))
        both = jnp.concatenate([hi[:, lanes], lo[:, lanes]], axis=1)
        below = jnp.concatenate([hi[:, lanes], jnp.zeros((depth, 128), BF)], axis=1)
        full = dot_nn(jnp.concatenate([left_hi, left_lo], axis=1), jnp.concatenate([both, below], axis=0))
        full = full[:, 0:128] + full[:, 128:256]
        out.append(jnp.where(low, full[0:rows], full[rows : 2 * rows]))
    return jnp.concatenate(out, axis=1)


def attend(work):
    scores, dprobs = [], []
    for key_l, value_l, query_r, cot_r, *_, bias_ref, _, _, _ in work:
        for head in range(HEADS):
            scores.append(dot_nt(key_l[head], query_r[head]) + bias_ref[...])
            dprobs.append(dot_nt(value_l[head], cot_r[head]))
    prob_rows, ds_rows, ds_cols = [], [], []
    for item, (*_, own_tokens, own_keys, inner) in enumerate(work):
        for head in range(HEADS):
            s, dp = scores[HEADS * item + head], dprobs[HEADS * item + head]
            top = jnp.maximum(jnp.max(s, axis=0, keepdims=True), -1e29)
            e = jnp.exp(s - top)
            inv = 1.0 / jnp.maximum(jnp.sum(e, axis=0, keepdims=True), 1e-30)
            delta = inv * jnp.sum(e * dp, axis=0, keepdims=True)
            prob_rows.append(e[0:own_keys] * inv)
            ds = [e[part] * inv * (dp[part] - delta) for part in inner]
            ds_rows.append(ds[0][0:own_keys])
            short = 128 - sum(x.shape[0] for x in ds)
            ds = jnp.concatenate(ds + [jnp.zeros((short, 128), F32)] * (short > 0), axis=0)
            ds_cols.append(ds[:, 0:own_tokens].T)
    out = []
    for item, (_, _, _, _, key, query, cot, *_) in enumerate(work):
        here = slice(HEADS * item, HEADS * item + HEADS)
        out.append((
            heads_product(ds_cols[here], key) * 0.125,
            heads_product(ds_rows[here], query),
            heads_product(prob_rows[here], cot),
        ))
    return out


def rows(ref, first, count, pad=0):
    x = ref[first : first + count, :]
    return [x, jnp.zeros((pad, 256), F32)] if pad else [x]


CORNER = (0, 36, 72, 81)
REST = (0, 12, 24, 39)
SIDE = (0, 48, 96, 120)


def keep(ref, image, parts):
    count = parts[0].shape[0]
    for head in range(HEADS):
        first = (HEADS * image + head) * count
        ref[first : first + count, :] = parts[head]


def joined(image, refs, late, rows):
    out = []
    for head in range(HEADS):
        parts = []
        for ref, take in refs:
            count = ref.shape[0] // (2 * HEADS)
            first = (HEADS * image + head) * count
            parts.append(ref[first : first + take, :])
        parts.append(late[head])
        have = sum(x.shape[0] for x in parts)
        if have < rows:
            parts.append(jnp.zeros((rows - have, late[head].shape[1]), BF))
        out.append(jnp.concatenate(parts, axis=0))
    return out


def own_kernel(cols, own_q_ref, own_k_ref, own_v_ref, own_c_ref, even_bias_ref, odd_bias_ref, k_ref, v_ref, q_ref, c_ref):
    at = Places(cols)
    write_bias(
        even_bias_ref,
        ((at.own, 64, 64), (at.ha_in, 24, 24), (at.ha_out, 24, 24), (at.even_inner, 24, 24), (at.even_outer, 24, 24),
         (at.mate_in, 24, 24), (at.deven_out, 24, 24)),
        ((None, 0, 24), (lambda i: at.own(i, 3), 40, 40), (lambda i: at.ha_in(i, 3), 15, 16), (at.even_inner, 24, 24),
         (at.deven_in, 24, 24)),
    )
    write_bias(
        odd_bias_ref,
        ((at.own, 48, 48), (at.ha_in, 18, 24), (at.ha_out, 18, 24), (at.odd_inner, 24, 24), (at.odd_outer, 24, 24),
         (at.dodd_in, 9, 16), (at.dodd_out, 27, 32)),
        ((at.own, 24, 32), (at.ha_in, 9, 16), (at.odd_tokens, 24, 32), (at.dodd_in, 9, 16)),
    )
    for image in range(2):
        here = slice(64 * image, 64 * image + 64)
        keep(k_ref, image, stacked(own_k_ref[here, :], True, 3))
        keep(v_ref, image, stacked(own_v_ref[here, :], True, 2))
        keep(q_ref, image, stacked(own_q_ref[here, :] * 0.125, False, 3))
        keep(c_ref, image, stacked(own_c_ref[here, :], False, 2))


def ha_inner(image, corner_ref, rest_ref, field):
    return rows(corner_ref, 90 * image + CORNER[field], 18) + rows(rest_ref, 54 * image + REST[field], 6)


def ha_outer(image, corner_ref, rest_ref, field):
    return rows(corner_ref, 90 * image + CORNER[field] + 18, 18) + rows(rest_ref, 54 * image + REST[field] + 6, 6)


def odd_inner(image, odd_ref, odd_rest_ref, field):
    corner, rest = 90 * image + CORNER[field], 54 * image + REST[field]
    return rows(odd_ref, corner, 9) + rows(odd_ref, corner + 18, 9) + rows(odd_rest_ref, rest, 6)


def odd_outer(image, odd_ref, odd_rest_ref, field):
    corner, rest = 90 * image + CORNER[field], 54 * image + REST[field]
    return rows(odd_ref, corner + 9, 9) + rows(odd_ref, corner + 27, 9) + rows(odd_rest_ref, rest + 6, 6)


def odd_middle_tokens(image, corner_ref, odd_ref, odd_rest_ref, field):
    corner, rest = 90 * image + CORNER[field], 54 * image + REST[field]
    return rows(corner_ref, corner, 9, 7) + rows(odd_ref, corner, 9) + rows(odd_rest_ref, rest, 15, 8)


def middle_kernel(corner_ref, rest_ref, odd_ref, odd_rest_ref, even_k_ref, even_v_ref, even_q_ref, even_c_ref,
                  odd_k_ref, odd_v_ref, odd_q_ref, odd_c_ref):
    for image in range(2):
        for field, even_ref, odd_to_ref, parts in ((0, even_k_ref, odd_k_ref, 3), (1, even_v_ref, odd_v_ref, 2)):
            corner = 90 * image + CORNER[field]
            x = ha_inner(image, corner_ref, rest_ref, field) + ha_outer(image, corner_ref, rest_ref, field)
            keep(even_ref, image, stacked(jnp.concatenate(x, axis=0), True, parts))
            x = rows(corner_ref, corner, 18, 6) + rows(corner_ref, corner + 18, 18, 6)
            x += odd_inner(image, odd_ref, odd_rest_ref, field) + odd_outer(image, odd_ref, odd_rest_ref, field)
            keep(odd_to_ref, image, stacked(jnp.concatenate(x, axis=0), True, parts))
        for field, even_ref, odd_to_ref, parts, scale in (
            (2, even_q_ref, odd_q_ref, 3, 0.125), (3, even_c_ref, odd_c_ref, 2, 1.0),
        ):
            x = jnp.concatenate(rows(rest_ref, 54 * image + REST[field], 15, 1), axis=0)
            keep(even_ref, image, stacked(x * scale, False, parts))
            x = jnp.concatenate(odd_middle_tokens(image, corner_ref, odd_ref, odd_rest_ref, field), axis=0)
            keep(odd_to_ref, image, stacked(x * scale, False, parts))


def even_work(own_q_ref, own_k_ref, own_c_ref, corner_ref, rest_ref, even_ref, mate_ref, bias_ref,
                k0_ref, v0_ref, q0_ref, c0_ref, k1_ref, v1_ref, q1_ref, c1_ref):
    work = []
    for image in range(2):

        def mate_inner(field):
            corner = 90 * image + CORNER[field]
            out = rows(mate_ref, corner + 9, 9) + rows(mate_ref, 184 + 54 * image + REST[field], 6)
            return out + rows(mate_ref, corner, 9)

        def late_keys(field):
            even = 144 * image + SIDE[field]
            out = rows(even_ref, even, 48) + mate_inner(field)
            out += rows(mate_ref, 90 * image + CORNER[field] + 18, 18)
            out += rows(mate_ref, 184 + 54 * image + REST[field] + 6, 6)
            return jnp.concatenate(out, axis=0)

        def late_tokens(field):
            out = rows(even_ref, 144 * image + SIDE[field], 24)
            out += rows(mate_ref, 90 * image + CORNER[field], 9) + rows(mate_ref, 184 + 54 * image + REST[field], 15)
            return jnp.concatenate(out, axis=0)

        late_q, late_c = late_tokens(2) * 0.125, late_tokens(3)
        key = rows(own_k_ref, 64 * image, 64) + ha_inner(image, corner_ref, rest_ref, 0)
        key += rows(even_ref, 144 * image, 24) + [jnp.concatenate(mate_inner(0), axis=0)[0:16]]
        query = rows(own_q_ref, 64 * image, 64) + rows(rest_ref, 54 * image + REST[2], 15, 1)
        cot = rows(own_c_ref, 64 * image, 64) + rows(rest_ref, 54 * image + REST[3], 15, 1)
        work.append((
            joined(image, ((k0_ref, 64), (k1_ref, 48)), stacked(late_keys(0), True, 3), 208),
            joined(image, ((v0_ref, 64), (v1_ref, 48)), stacked(late_keys(1), True, 2), 208),
            joined(image, ((q0_ref, 64), (q1_ref, 16)), stacked(late_q, False, 3), 128),
            joined(image, ((c0_ref, 64), (c1_ref, 16)), stacked(late_c, False, 2), 128),
            jnp.concatenate(key, axis=0),
            jnp.concatenate([jnp.concatenate(query, axis=0) * 0.125, late_q], axis=0),
            jnp.concatenate(cot + [late_c], axis=0),
            bias_ref, 64, 64, (slice(0, 88), slice(112, 136), slice(160, 176)),
        ))
    return work


def sort_kernel(cols, first_ref, second_ref, rest_ref, gate_ref, ha_ref, odd_ref, mate_ref):
    turned = by_row(lax.axis_index("wa"), cols)
    first, second = first_ref[...], second_ref[...]
    ha = jnp.where(turned, second, first)
    ha_ref[...] = ha
    odd_ref[...] = jnp.where(turned, first, second)
    mate_ref[0:184, :] = ha
    mate_ref[184:296, :] = rest_ref[...]


def release_kernel(message_ref, gate_ref, out_ref):
    out_ref[...] = message_ref[...]


def by_row(w, cols):
    return jnp.logical_and(((w + 1) >> 1) % 2 == 0, jnp.logical_and(w > 0, w < cols - 1))


def odd_work(own_q_ref, own_k_ref, own_c_ref, corner_ref, odd_ref, odd_rest_ref, far_ref, bias_ref, k0_ref, v0_ref, q0_ref, c0_ref, k1_ref, v1_ref, q1_ref, c1_ref):
    work = []
    for image in range(2):

        def late_keys(field):
            corner = 90 * image + CORNER[field]
            return jnp.concatenate(rows(far_ref, corner, 9, 7) + rows(far_ref, corner + 9, 27, 5), axis=0)

        def late_tokens(field):
            return jnp.concatenate(rows(far_ref, 90 * image + CORNER[field], 9, 7), axis=0)

        late_q, late_c = late_tokens(2) * 0.125, late_tokens(3)
        late_k = late_keys(0)
        key = rows(own_k_ref, 64 * image, 48) + rows(corner_ref, 90 * image, 18, 6)
        key += odd_inner(image, odd_ref, odd_rest_ref, 0) + [late_k[0:16]]
        query = rows(own_q_ref, 64 * image, 32) + odd_middle_tokens(image, corner_ref, odd_ref, odd_rest_ref, 2)
        cot = rows(own_c_ref, 64 * image, 32) + odd_middle_tokens(image, corner_ref, odd_ref, odd_rest_ref, 3)
        work.append((
            joined(image, ((k0_ref, 48), (k1_ref, 96)), stacked(late_k, True, 3), 192),
            joined(image, ((v0_ref, 48), (v1_ref, 96)), stacked(late_keys(1), True, 2), 192),
            joined(image, ((q0_ref, 32), (q1_ref, 48)), stacked(late_q, False, 3), 128),
            joined(image, ((c0_ref, 32), (c1_ref, 48)), stacked(late_c, False, 2), 128),
            jnp.concatenate(key, axis=0),
            jnp.concatenate([jnp.concatenate(query, axis=0) * 0.125, late_q], axis=0),
            jnp.concatenate(cot + [late_c], axis=0),
            bias_ref, 24, 48, (slice(0, 72), slice(96, 120), slice(144, 160)),
        ))
    return work


def last_kernel(own_q_ref, own_k_ref, own_c_ref, corner_ref, rest_ref, even_ref, mate_ref, odd_ref, odd_rest_ref, far_ref,
                even_bias_ref, odd_bias_ref, k0_ref, v0_ref, q0_ref, c0_ref, k1_ref, v1_ref, q1_ref, c1_ref,
                k2_ref, v2_ref, q2_ref, c2_ref, dq_ref, dk_ref, dv_ref, split_ref):
    p = lax.axis_index("wa") % 2
    own = (own_q_ref, own_k_ref, own_c_ref)
    kept = (k0_ref, v0_ref, q0_ref, c0_ref)
    work = even_work(*own, corner_ref, rest_ref, even_ref, mate_ref, even_bias_ref, *kept, k1_ref, v1_ref, q1_ref, c1_ref)
    work += odd_work(*own, corner_ref, odd_ref, odd_rest_ref, far_ref, odd_bias_ref, *kept, k2_ref, v2_ref, q2_ref, c2_ref)
    parts = attend(work)
    for image in range(2):
        even_dq, even_dk, even_dv = parts[image]
        dq, dk, dv = parts[2 + image]
        none = jnp.zeros((16, 256), F32)
        results = (
            jnp.concatenate([dq, jnp.zeros((40, 256), F32)], axis=0) + even_dq,
            jnp.concatenate([dk, none], axis=0) + even_dk,
            jnp.concatenate([dv, none], axis=0) + even_dv,
        )
        for index, x in enumerate(results):
            for slot in range(8):
                where = pl.ds(64 * image + slot_column(p, slot), 8, stride=8)
                for half in range(2):
                    split_ref[2 * index + half, where, :] = x[8 * slot : 8 * slot + 8, 128 * half : 128 * half + 128]
    for index, ref in enumerate((dq_ref, dk_ref, dv_ref)):
        for half in range(2):
            ref[:, 128 * half : 128 * half + 128] = split_ref[2 * index + half, 0:128, :]


SMALL = pltpu.CompilerParams(vmem_limit_bytes=6 * 1024 * 1024)
LARGE = pltpu.CompilerParams(vmem_limit_bytes=12 * 1024 * 1024)
OWN_US = 0
PREP_US = 1.5
FAR_US = 2


def cost(micros):
    return pl.CostEstimate(flops=int(micros * 1e9), bytes_accessed=int(micros * 3e6), transcendentals=0)


def per_device(queries, keys, values, cotangent):
    shape = queries.shape
    cols = lax.axis_size("wa")
    flat = [x.reshape(128, 256) for x in (queries, keys, values, cotangent)]
    to_corner, split = pl.pallas_call(
        corner_kernel, out_shape=(vmem(184), pltpu.VMEM((8, SPLIT, 128), F32)), name="corner",
    )(flat[1], flat[2], flat[0], flat[3])
    to_rest, to_odd_rest, to_even, own_k, own_v, own_q, own_c = pl.pallas_call(
        pack_kernel, out_shape=(vmem(112), vmem(112), vmem(288)) + (vmem(128),) * 4, name="pack", compiler_params=SMALL,
    )(held(split))
    own = (own_q, own_k, own_v, own_c)

    both = ("ha", "wa")
    ends = (0, cols - 1)
    partner = {i: (i + 1 if i % 2 else i - 1) for i in range(cols) if i not in ends}
    first_pairs, second_pairs, far_pairs, odd_pairs = [], [], [], []
    for row in range(2):
        for col in range(cols):
            here, mate = row * cols + col, (1 - row) * cols + col
            beside = mate if col in ends else row * cols + partner[col]
            turned = (col + 1) // 2 % 2 == 0
            first_pairs.append((here, beside if turned else mate))
            far_pairs.append((here, mate if turned else beside))
            second_pairs.append((here, here if col in ends else mate if turned else beside))
            odd_pairs.append((here, beside))
    even_pairs = [(i, i ^ 1) for i in range(cols)]
    across = [(0, 1), (1, 0)]

    first = lax.ppermute(to_corner, both, first_pairs)
    second = lax.ppermute(to_corner, both, second_pairs)
    rest = lax.ppermute(to_rest, "ha", across)
    odd_rest = lax.ppermute(to_odd_rest, both, odd_pairs)
    to_even = pl.pallas_call(release_kernel, out_shape=vmem(288), name="release", compiler_params=SMALL)(held(to_even), held(first))
    even = lax.ppermute(to_even, "wa", even_pairs)
    far = lax.ppermute(first, both, far_pairs)
    each = 2 * HEADS

    def stacks(key_rows, token_rows):
        return (vmem(each * key_rows, 384, BF), vmem(each * key_rows, 256, BF), vmem(each * token_rows, 384, BF),
                vmem(each * token_rows, 256, BF))

    even_bias, odd_bias, *own_stacks = pl.pallas_call(
        functools.partial(own_kernel, cols),
        out_shape=(vmem(208, 128), vmem(192, 128)) + stacks(64, 64),
        compiler_params=SMALL,
        cost_estimate=cost(OWN_US),
        name="own",
    )(*[held(x) for x in own])
    corner, odd, to_mate = pl.pallas_call(
        functools.partial(sort_kernel, cols), out_shape=(vmem(184), vmem(184), vmem(296)), name="sort", compiler_params=SMALL,
    )(*[held(x) for x in (first, second, rest, even_bias)])
    mate = lax.ppermute(to_mate, "wa", even_pairs)
    middle = pl.pallas_call(
        middle_kernel,
        out_shape=stacks(48, 16) + stacks(96, 48),
        compiler_params=SMALL,
        cost_estimate=cost(PREP_US),
        name="middle",
    )(*[held(x) for x in (corner, rest, odd, odd_rest)])
    if FAR_US:
        far = pl.pallas_call(
            release_kernel, out_shape=vmem(184), cost_estimate=cost(FAR_US), name="arrive_far", compiler_params=SMALL,
        )(held(far), held(first))
    out = jax.ShapeDtypeStruct((128, 256), F32)
    grads = pl.pallas_call(
        last_kernel,
        out_shape=(out, out, out),
        scratch_shapes=[pltpu.VMEM((6, SPLIT, 128), F32)],
        compiler_params=LARGE,
        name="attend",
    )(*[held(x) for x in (own_q, own_k, own_c, corner, rest, even, mate, odd, odd_rest, far, even_bias, odd_bias,
                          *own_stacks, *middle)])
    return tuple(g.reshape(shape) for g in grads)


def solution(mesh):
    spec = P(None, "ha", "wa", None)
    return jax.shard_map(
        per_device,
        mesh=mesh,
        in_specs=(spec,) * 4,
        out_specs=(spec,) * 3,
        check_vma=False,
    )
```
